512 devices in a mesh: tok: 32 (over x, y, core), fsdp: 16 (over z).
Axes of the slice: x: 4, y: 4, z: 16, core: 2. Of those that a mesh axis runs over, the one named last changes fastest.
Arguments:
- hidden: bfloat16 [65536, 4096], P(('fsdp', 'tok')), may hold values from -6 to 6
- queries: bfloat16 [65536, 4096], P(('fsdp', 'tok')), may hold values from -64 to 64
- upstream: bfloat16 [65536, 4096], P(('fsdp', 'tok')), may hold values from -6 to 6
- context_weight: bfloat16 [4096, 1024], P('fsdp'), may hold values from -0.09375 to 0.09375
- lengths: int32 [16, 16], P('fsdp'), may hold values from 1 to 512, 4096 in all within a row
Outputs:
- log_totals: float32 [32, 65536], P(None, ('fsdp', 'tok'))
- query_slopes: bfloat16 [65536, 4096], P(('fsdp', 'tok'))
- context_slopes: bfloat16 [65536, 1024], P(('fsdp', 'tok'))
The draws below stay inside these ranges and needn't reach their ends.
Inputs may be any that keep to these rules, and one draw needn't show every extreme that they name: Row p holds the lengths of pack p's documents in order; each row sums to 4096 and its longest document has exactly 512 tokens.
All inputs are finite; a program needn't handle non-finite values.
Results may differ from the reference program's by a relative error of at most 0.03.
The reference program's roundings to bfloat16 on the way count: a program that leaves them out, or rounds other values in their place, can miss the bound.
Values may be sent and summed in bfloat16 or wider, within the bound.
No kernel may reach another device: no remote copies, remote signals or barrier semaphores. Data moves between devices by JAX's collectives and lax.ppermute only.
A program may use at most 64 MiB of HBM per device.

```python
import math
import jax
import jax.numpy as jnp
import numpy as np
from jax import lax

D = 4096
QH = 32
KVH = 4
HD = 128
MAXDOC = 512
SEQ = 4096
DOCS = 16
TOKENS = 65536
N_FSDP = 16


def draw_queries(key, part):
    key = jax.random.fold_in(key, 11)
    values = jnp.clip(jax.random.normal(key, (TOKENS, QH * HD), jnp.float32), -6.0, 6.0)
    return values.astype(jnp.bfloat16)


def levels(own_key, extent, shards, low, high):
    loudness = 1.0
    for position, parts in shards:
        heights = jax.random.uniform(jax.random.fold_in(jax.random.fold_in(own_key, 6), position), (parts,), jnp.float32, low / len(shards), high / len(shards))
        loudness = loudness * jnp.repeat(jnp.exp(heights), extent[position] // parts).reshape((-1,) + (1,) * (len(extent) - 1 - position))
    return loudness


def split_up(count, total, bound, slope):
    portions = [(1 << 20) // math.isqrt(grade ** slope) + 1 for grade in range(2, count + 1)]
    spare, counts = total - bound - (count - 1), [1] * (count - 1)
    while spare > 0:
        movable = [i for i in range(count - 1) if counts[i] < bound]
        mass, remaining = sum([portions[i] for i in movable]), spare
        for i in movable:
            addition = min(bound - counts[i], max(1, remaining * portions[i] // mass), spare)
            counts[i] = counts[i] + addition
            spare = spare - addition
    return np.array([bound] + counts)


def ragged(rng, amount, total, reach, slope):
    if amount == 2:
        one = jax.random.randint(rng, (), max(1, total - reach), min(reach, total - 1) + 1)
        return jnp.stack([one, total - one])
    sizes = jnp.asarray(split_up(amount, total, reach, slope), jnp.int32)
    pairs = (amount - 1) // 2
    giver, sink = sizes[1:1 + 2 * pairs:2], sizes[2:2 + 2 * pairs:2]
    margin = jnp.minimum(giver - 1, reach - sink)
    moved = jax.random.randint(jax.random.fold_in(rng, 1), (pairs,), 0, 1 << 20) % (margin + 1)
    sizes = sizes.at[1:1 + 2 * pairs:2].set(giver - moved).at[2:2 + 2 * pairs:2].set(sink + moved)
    return sizes[jax.random.permutation(jax.random.fold_in(rng, 2), amount)]


def noise(own_key, extent, scale, reach, shards=(), kind=jnp.bfloat16):
    array = scale * jax.random.normal(own_key, extent, jnp.float32)
    if shards:
        array = array * levels(own_key, extent, shards, -0.22, 0.18)
    return jnp.clip(array, -reach, reach).astype(kind)


def setup_inputs(seed: int = 0) -> dict:
    seeds = jax.random.split(jax.random.key(seed), 6)
    hidden = noise(seeds[0], (TOKENS, D), 1.0, 6.0, ((0, 512),))
    queries = draw_queries(jax.random.fold_in(seeds[5], 71), 0)
    upstream = noise(seeds[2], (TOKENS, QH * HD), 1.0, 6.0, ((0, 512),))
    context_weight = noise(seeds[3], (D, 2 * KVH * HD), D ** -0.5, 0.09375, ((0, 16),))
    lengths = jax.vmap(lambda own: ragged(own, DOCS, SEQ, MAXDOC, 2))(jax.random.split(seeds[4], N_FSDP)).reshape((N_FSDP, DOCS)).astype(jnp.int32)
    return dict(hidden=hidden, queries=queries, upstream=upstream, context_weight=context_weight, lengths=lengths)


def document_of(places, bounds):
    return lax.optimization_barrier(jnp.sum((places[:, None] >= bounds[None, :]).astype(jnp.int32), axis=1))

def permitted(query_places, key_places, bounds):
    same_document = document_of(query_places, bounds)[:, None] == document_of(key_places, bounds)[None, :]
    return same_document & (key_places[None, :] >= 0) & (key_places[None, :] <= query_places[:, None])

def attend(query_block, key_block, value_block, upstream_block, allowed, score_scale):
    query_wide = query_block.astype(jnp.float32)
    key_wide = key_block.astype(jnp.float32)
    value_wide = value_block.astype(jnp.float32)
    upstream_wide = upstream_block.astype(jnp.float32)
    scores = jnp.einsum('rkge,cke->kgrc', query_wide, key_wide) * score_scale
    scores = jnp.where(allowed, scores, -jnp.inf)
    highest = lax.optimization_barrier(jnp.max(scores, axis=-1))
    totals = lax.optimization_barrier(jnp.sum(jnp.exp(scores - highest[..., None]), axis=-1))
    log_total = highest + jnp.log(totals)
    weights = jnp.exp(scores - log_total[..., None])
    rounded = weights.astype(jnp.bfloat16).astype(jnp.float32)
    attended = lax.optimization_barrier(jnp.einsum('kgrc,cke->rkge', rounded, value_wide).astype(jnp.bfloat16))
    inner_sum = lax.optimization_barrier(jnp.sum(upstream_wide * attended.astype(jnp.float32), axis=-1))
    pushed = jnp.einsum('rkge,cke->kgrc', upstream_wide, value_wide)
    score_change = (weights * (pushed - jnp.transpose(inner_sum, (1, 2, 0))[..., None])).astype(jnp.bfloat16).astype(jnp.float32)
    query_slope = jnp.einsum('kgrc,cke->rkge', score_change, key_wide) * score_scale
    key_slope = jnp.einsum('kgrc,rkge->cke', score_change, query_wide) * score_scale
    value_slope = jnp.einsum('kgrc,rkge->cke', rounded, upstream_wide)
    return (log_total, query_slope, key_slope, value_slope)

def reference(hidden, queries, upstream, context_weight, lengths):
    group_size = QH // KVH
    score_scale = 1.0 / math.sqrt(HD)
    block_rows = MAXDOC
    block_total = SEQ // MAXDOC

    def one_pack(pack_items):
        hidden_pack, queries_pack, upstream_pack, pack_lengths = pack_items
        context = jnp.dot(hidden_pack, context_weight, preferred_element_type=jnp.float32).astype(jnp.bfloat16)
        bounds = jnp.cumsum(pack_lengths).astype(jnp.int32)
        padded = jnp.concatenate([jnp.zeros((block_rows, 2 * KVH * HD), jnp.bfloat16), context], axis=0)

        def one_block(running, number):
            first_row = number * block_rows
            query_block = lax.dynamic_slice_in_dim(queries_pack, first_row, block_rows, 0).reshape(block_rows, KVH, group_size, HD)
            upstream_block = lax.dynamic_slice_in_dim(upstream_pack, first_row, block_rows, 0).reshape(block_rows, KVH, group_size, HD)
            window = lax.dynamic_slice_in_dim(padded, first_row, 2 * block_rows, 0).reshape(2 * block_rows, 2, KVH, HD)
            query_places = first_row + jnp.arange(block_rows, dtype=jnp.int32)
            key_places = first_row - block_rows + jnp.arange(2 * block_rows, dtype=jnp.int32)
            allowed = permitted(query_places, key_places, bounds)
            log_total, query_slope, key_slope, value_slope = attend(query_block, window[:, 0], window[:, 1], upstream_block, allowed, score_scale)
            update = jnp.concatenate([key_slope.reshape(2 * block_rows, KVH * HD), value_slope.reshape(2 * block_rows, KVH * HD)], axis=1)
            current = lax.dynamic_slice_in_dim(running, first_row, 2 * block_rows, 0)
            running = lax.dynamic_update_slice_in_dim(running, current + update, first_row, 0)
            return (running, (log_total.reshape(QH, block_rows), query_slope.reshape(block_rows, QH * HD).astype(jnp.bfloat16)))
        initial = jnp.zeros((SEQ + block_rows, 2 * KVH * HD), jnp.float32)
        summed, (totals, slopes) = lax.scan(one_block, initial, jnp.arange(block_total, dtype=jnp.int32))
        log_pack = jnp.transpose(totals, (1, 0, 2)).reshape(QH, SEQ)
        return (log_pack, slopes.reshape(SEQ, QH * HD), summed[block_rows:].astype(jnp.bfloat16))
    log_all, query_all, context_all = lax.map(one_pack, (hidden.reshape(N_FSDP, SEQ, D), queries.reshape(N_FSDP, SEQ, QH * HD), upstream.reshape(N_FSDP, SEQ, QH * HD), lengths))
    log_totals = jnp.transpose(log_all, (1, 0, 2)).reshape(QH, N_FSDP * SEQ)
    return (log_totals, query_all.reshape(N_FSDP * SEQ, QH * HD), context_all.reshape(N_FSDP * SEQ, 2 * KVH * HD))
```

```python
import functools
import math

import jax
import jax.numpy as jnp
from jax import lax
from jax.experimental import pallas as pl
from jax.experimental.pallas import tpu as pltpu
from jax.sharding import PartitionSpec as P

QH = 32
KVH = 4
HD = 128
CORES = 2
BLOCK = 128
CHIP = CORES * BLOCK
GROUPS = KVH // CORES
HEADS = QH // KVH
SPAN = 4 * BLOCK
KEYS = SPAN + BLOCK
SCALE = 1.0 / math.sqrt(HD)
LOG2E = math.log2(math.e)


def shifted(block, distance):
    count = lax.axis_size("tok")
    route = [(i, i + distance) for i in range(count) if 0 <= i + distance < count]
    return lax.ppermute(block, "tok", route)


def swapped(block):
    count = lax.axis_size("tok")
    return lax.ppermute(block, "tok", [(i, i ^ 1) for i in range(count)])


def by_core(core, mine, other, axis):
    return jnp.where(
        core == 0,
        jnp.concatenate([mine, other], axis=axis),
        jnp.concatenate([other, mine], axis=axis),
    )


def half(block, index, axis):
    size = block.shape[axis] // 2
    return lax.dynamic_slice_in_dim(block, index * size, size, axis)


def attention_kernel(
    start_ref, q_ref, qt_ref, u_ref, ut_ref, far_ref, near_ref, here_ref,
    log_ref, dq_ref, dfar_ref, dnear_ref, dhere_ref,
    keys, values, sums, bias, weight_rows, change_rows,
):
    part = pl.program_id(1)

    @pl.when(part == 0)
    def _():
        for i, ref in enumerate((far_ref, near_ref, here_ref)):
            keys[i * CHIP : (i + 1) * CHIP, :] = ref[:, :HD]
            values[i * CHIP : (i + 1) * CHIP, :] = ref[:, HD:]
        sums[...] = jnp.zeros_like(sums)

    first = pl.multiple_of(part * BLOCK, BLOCK)
    key_window = keys[pl.ds(first, KEYS), :]
    value_window = values[pl.ds(first, KEYS), :]
    places = first - SPAN + lax.broadcasted_iota(jnp.int32, (BLOCK, KEYS), 1)
    own = first + lax.broadcasted_iota(jnp.int32, (BLOCK, KEYS), 0)
    bias[...] = jnp.where((places <= own) & (places >= start_ref[...]), 0.0, -jnp.inf)
    logs = jnp.zeros((BLOCK, HD), jnp.float32)
    lane = lax.broadcasted_iota(jnp.int32, (BLOCK, HD), 1)
    over_rows = (((1,), (1,)), ((), ()))
    for pair in range(HEADS // 2):
        rows = slice(pair * 2 * BLOCK, (pair + 1) * 2 * BLOCK)
        scores = lax.dot_general(
            q_ref[0, 0, rows, :], key_window, over_rows, preferred_element_type=jnp.float32
        )
        scores = scores + jnp.concatenate([bias[...], bias[...]], axis=0)
        highest = jnp.max(scores, axis=1, keepdims=True)
        raised = jnp.exp2((scores - highest) * (SCALE * LOG2E))
        total = jnp.sum(raised, axis=1, keepdims=True)
        log_total = highest * SCALE + jnp.log(total)
        weights = raised * (1.0 / total)
        rounded = weights.astype(jnp.bfloat16)
        weight_rows[rows, :] = rounded
        attended = jnp.dot(rounded, value_window, preferred_element_type=jnp.float32)
        attended = attended.astype(jnp.bfloat16).astype(jnp.float32)
        upstream = u_ref[0, 0, rows, :]
        inner = jnp.sum(upstream.astype(jnp.float32) * attended, axis=1, keepdims=True)
        pushed = lax.dot_general(
            upstream, value_window, over_rows, preferred_element_type=jnp.float32
        )
        change = (weights * (pushed - inner)).astype(jnp.bfloat16)
        change_rows[rows, :] = change
        slope = jnp.dot(change, key_window, preferred_element_type=jnp.float32) * SCALE
        for i in range(2):
            head = pair * 2 + i
            part_rows = slice(i * BLOCK, (i + 1) * BLOCK)
            dq_ref[:, head * HD : (head + 1) * HD] = slope[part_rows].astype(jnp.bfloat16)
            logs = jnp.where(lane == head, log_total[part_rows], logs)
    log_ref[0] = logs.T[:HEADS]
    key_slope = jnp.dot(qt_ref[0, 0], change_rows[...], preferred_element_type=jnp.float32)
    value_slope = jnp.dot(ut_ref[0, 0], weight_rows[...], preferred_element_type=jnp.float32)
    sums[pl.ds(first, KEYS), :HD] += key_slope.T * SCALE
    sums[pl.ds(first, KEYS), HD:] += value_slope.T

    @pl.when(part == CORES - 1)
    def _():
        for i, ref in enumerate((dfar_ref, dnear_ref, dhere_ref)):
            ref[...] = sums[i * CHIP : (i + 1) * CHIP, :].astype(ref.dtype)


def attention(starts, q, qt, u, ut, far, near, here):
    stacked = HEADS * BLOCK
    rows = pl.BlockSpec((1, 1, stacked, HD), lambda g, b: (b, g, 0, 0))
    columns = pl.BlockSpec((1, 1, HD, stacked), lambda g, b: (b, g, 0, 0))
    context = pl.BlockSpec((CHIP, 2 * HD), lambda g, b: (0, g))
    wide = GROUPS * 2 * HD
    return pl.pallas_call(
        attention_kernel,
        grid=(GROUPS, CORES),
        in_specs=[
            pl.BlockSpec((BLOCK, 1), lambda g, b: (b, 0)),
            rows, columns, rows, columns, context, context, context,
        ],
        out_specs=[
            pl.BlockSpec((1, HEADS, BLOCK), lambda g, b: (b, g, 0)),
            pl.BlockSpec((BLOCK, HEADS * HD), lambda g, b: (b, g)),
            context, context, context,
        ],
        out_shape=[
            jax.ShapeDtypeStruct((CORES, GROUPS * HEADS, BLOCK), jnp.float32),
            jax.ShapeDtypeStruct((CHIP, GROUPS * HEADS * HD), jnp.bfloat16),
            jax.ShapeDtypeStruct((CHIP, wide), jnp.bfloat16),
            jax.ShapeDtypeStruct((CHIP, wide), jnp.bfloat16),
            jax.ShapeDtypeStruct((CHIP, wide), jnp.float32),
        ],
        scratch_shapes=[
            pltpu.VMEM((SPAN + CHIP, HD), jnp.bfloat16),
            pltpu.VMEM((SPAN + CHIP, HD), jnp.bfloat16),
            pltpu.VMEM((SPAN + CHIP, 2 * HD), jnp.float32),
            pltpu.VMEM((BLOCK, KEYS), jnp.float32),
            pltpu.VMEM((stacked, KEYS), jnp.bfloat16),
            pltpu.VMEM((stacked, KEYS), jnp.bfloat16),
        ],
        compiler_params=pltpu.CompilerParams(vmem_limit_bytes=48 * 2**20),
        cost_estimate=pl.CostEstimate(
            flops=12 * CHIP * KEYS * HD * GROUPS * HEADS,
            bytes_accessed=8 * 2**20,
            transcendentals=CHIP * KEYS * GROUPS * HEADS,
        ),
        name="attention",
    )(starts, q, qt, u, ut, far, near, here)


def body(hidden, queries, upstream, context_weight, lengths):
    device = lax.axis_index("tok")
    core, chip = device % CORES, device // CORES
    ordered = context_weight.reshape(-1, 2, CORES, GROUPS, HD)
    ordered = lax.dynamic_slice_in_dim(ordered, core, 1, 2)[:, :, 0]
    ordered = ordered.transpose(0, 2, 1, 3).reshape(-1, GROUPS * 2 * HD)
    weight = lax.all_gather(ordered, "fsdp", axis=0, tiled=True)

    both = by_core(core, hidden, swapped(hidden), 0)

    def heads_of(block):
        mine = half(block, core, 1)
        other = swapped(half(block, 1 - core, 1))
        whole = by_core(core, mine, other, 0).reshape(CORES, BLOCK, GROUPS, HEADS, HD)
        rows = whole.transpose(0, 2, 3, 1, 4).reshape(CORES, GROUPS, HEADS * BLOCK, HD)
        columns = whole.transpose(0, 2, 4, 3, 1).reshape(CORES, GROUPS, HD, HEADS * BLOCK)
        return rows, columns

    q, qt = heads_of(queries)
    u, ut = heads_of(upstream)
    bounds = jnp.cumsum(lengths[0])
    places = chip * CHIP + jnp.arange(CHIP, dtype=jnp.int32)
    starts = jnp.max(jnp.where(bounds[None, :] <= places[:, None], bounds[None, :], 0), axis=1)
    starts = (starts - chip * CHIP).astype(jnp.int32)[:, None]

    here = jnp.dot(both, weight, preferred_element_type=jnp.float32).astype(jnp.bfloat16)
    near = shifted(here, CORES)
    far = shifted(here, 2 * CORES)
    logs, dq, dfar, dnear, dhere = attention(starts, q, qt, u, ut, far, near, here)

    context_slopes = (
        dhere
        + shifted(dnear, -CORES).astype(jnp.float32)
        + shifted(dfar, -2 * CORES).astype(jnp.float32)
    ).astype(jnp.bfloat16)
    query_slopes = by_core(core, half(dq, core, 0), swapped(half(dq, 1 - core, 0)), 1)
    log_totals = by_core(core, half(logs, core, 0)[0], swapped(half(logs, 1 - core, 0)[0]), 0)
    context_slopes = by_core(
        core, half(context_slopes, core, 0), swapped(half(context_slopes, 1 - core, 0)), 1
    )
    context_slopes = context_slopes.reshape(BLOCK, KVH, 2, HD).transpose(0, 2, 1, 3)
    return log_totals, query_slopes, context_slopes.reshape(BLOCK, 2 * KVH * HD)


def solution(mesh):
    in_specs = (
        P(("fsdp", "tok"), None),
        P(("fsdp", "tok"), None),
        P(("fsdp", "tok"), None),
        P("fsdp", None),
        P("fsdp", None),
    )
    out_specs = (P(None, ("fsdp", "tok")), P(("fsdp", "tok"), None), P(("fsdp", "tok"), None))
    return jax.shard_map(body, mesh=mesh, in_specs=in_specs, out_specs=out_specs, check_vma=False)
```

```python
import functools
import math

import jax
import jax.numpy as jnp
from jax import lax
from jax.experimental import pallas as pl
from jax.experimental.pallas import tpu as pltpu
from jax.sharding import PartitionSpec as P

QH = 32
KVH = 4
HD = 128
CORES = 2
BLOCK = 128
CHIP = CORES * BLOCK
GROUPS = KVH // CORES
HEADS = QH // KVH
SPAN = 4 * BLOCK
KEYS = SPAN + BLOCK
SHARDS = 16
SLICES = 16
ROWS = 16
SCALE = 1.0 / math.sqrt(HD)
LOG2E = math.log2(math.e)


def shifted(block, distance):
    count = lax.axis_size("tok")
    route = [(i, i + distance) for i in range(count) if 0 <= i + distance < count]
    return lax.ppermute(block, "tok", route)


def swapped(block):
    count = lax.axis_size("tok")
    return lax.ppermute(block, "tok", [(i, i ^ 1) for i in range(count)])


def by_core(core, mine, other, axis):
    return jnp.where(
        core == 0,
        jnp.concatenate([mine, other], axis=axis),
        jnp.concatenate([other, mine], axis=axis),
    )


def half(block, index, axis):
    size = block.shape[axis] // 2
    return lax.dynamic_slice_in_dim(block, index * size, size, axis)


def attention_kernel(
    start_ref, q_ref, qt_ref, u_ref, ut_ref, far_ref, near_ref, here_ref,
    log_ref, dq_ref, dfar_ref, dnear_ref, dhere_ref,
    keys, values, sums, bias, weight_rows, change_rows,
):
    part = pl.program_id(1)

    @pl.when(part == 0)
    def _():
        for i, ref in enumerate((far_ref, near_ref, here_ref)):
            keys[i * CHIP : (i + 1) * CHIP, :] = ref[:, :HD]
            values[i * CHIP : (i + 1) * CHIP, :] = ref[:, HD:]
        sums[...] = jnp.zeros_like(sums)

    first = pl.multiple_of(part * BLOCK, BLOCK)
    key_window = keys[pl.ds(first, KEYS), :]
    value_window = values[pl.ds(first, KEYS), :]
    places = first - SPAN + lax.broadcasted_iota(jnp.int32, (BLOCK, KEYS), 1)
    own = first + lax.broadcasted_iota(jnp.int32, (BLOCK, KEYS), 0)
    bias[...] = jnp.where((places <= own) & (places >= start_ref[...]), 0.0, -jnp.inf)
    logs = jnp.zeros((BLOCK, HD), jnp.float32)
    lane = lax.broadcasted_iota(jnp.int32, (BLOCK, HD), 1)
    over_rows = (((1,), (1,)), ((), ()))
    for pair in range(HEADS // 2):
        rows = slice(pair * 2 * BLOCK, (pair + 1) * 2 * BLOCK)
        scores = lax.dot_general(
            q_ref[0, 0, rows, :], key_window, over_rows, preferred_element_type=jnp.float32
        )
        scores = scores + jnp.concatenate([bias[...], bias[...]], axis=0)
        highest = jnp.max(scores, axis=1, keepdims=True)
        raised = jnp.exp2((scores - highest) * (SCALE * LOG2E))
        total = jnp.sum(raised, axis=1, keepdims=True)
        log_total = highest * SCALE + jnp.log(total)
        weights = raised * (1.0 / total)
        rounded = weights.astype(jnp.bfloat16)
        weight_rows[rows, :] = rounded
        attended = jnp.dot(rounded, value_window, preferred_element_type=jnp.float32)
        attended = attended.astype(jnp.bfloat16).astype(jnp.float32)
        upstream = u_ref[0, 0, rows, :]
        inner = jnp.sum(upstream.astype(jnp.float32) * attended, axis=1, keepdims=True)
        pushed = lax.dot_general(
            upstream, value_window, over_rows, preferred_element_type=jnp.float32
        )
        change = (weights * (pushed - inner)).astype(jnp.bfloat16)
        change_rows[rows, :] = change
        slope = jnp.dot(change, key_window, preferred_element_type=jnp.float32) * SCALE
        for i in range(2):
            head = pair * 2 + i
            part_rows = slice(i * BLOCK, (i + 1) * BLOCK)
            dq_ref[:, head * HD : (head + 1) * HD] = slope[part_rows].astype(jnp.bfloat16)
            logs = jnp.where(lane == head, log_total[part_rows], logs)
    log_ref[0] = logs.T[:HEADS]
    key_slope = jnp.dot(qt_ref[0, 0], change_rows[...], preferred_element_type=jnp.float32)
    value_slope = jnp.dot(ut_ref[0, 0], weight_rows[...], preferred_element_type=jnp.float32)
    sums[pl.ds(first, KEYS), :HD] += key_slope.T * SCALE
    sums[pl.ds(first, KEYS), HD:] += value_slope.T

    @pl.when(part == CORES - 1)
    def _():
        for i, ref in enumerate((dfar_ref, dnear_ref, dhere_ref)):
            ref[...] = sums[i * CHIP : (i + 1) * CHIP, :].astype(ref.dtype)


def attention(starts, q, qt, u, ut, far, near, here):
    stacked = HEADS * BLOCK
    rows = pl.BlockSpec((1, 1, stacked, HD), lambda g, b: (b, g, 0, 0))
    columns = pl.BlockSpec((1, 1, HD, stacked), lambda g, b: (b, g, 0, 0))
    context = pl.BlockSpec((CHIP, 2 * HD), lambda g, b: (0, g))
    wide = GROUPS * 2 * HD
    return pl.pallas_call(
        attention_kernel,
        grid=(GROUPS, CORES),
        in_specs=[
            pl.BlockSpec((BLOCK, 1), lambda g, b: (b, 0)),
            rows, columns, rows, columns, context, context, context,
        ],
        out_specs=[
            pl.BlockSpec((1, HEADS, BLOCK), lambda g, b: (b, g, 0)),
            pl.BlockSpec((BLOCK, HEADS * HD), lambda g, b: (b, g)),
            context, context, context,
        ],
        out_shape=[
            jax.ShapeDtypeStruct((CORES, GROUPS * HEADS, BLOCK), jnp.float32),
            jax.ShapeDtypeStruct((CHIP, GROUPS * HEADS * HD), jnp.bfloat16),
            jax.ShapeDtypeStruct((CHIP, wide), jnp.bfloat16),
            jax.ShapeDtypeStruct((CHIP, wide), jnp.bfloat16),
            jax.ShapeDtypeStruct((CHIP, wide), jnp.float32),
        ],
        scratch_shapes=[
            pltpu.VMEM((SPAN + CHIP, HD), jnp.bfloat16),
            pltpu.VMEM((SPAN + CHIP, HD), jnp.bfloat16),
            pltpu.VMEM((SPAN + CHIP, 2 * HD), jnp.float32),
            pltpu.VMEM((BLOCK, KEYS), jnp.float32),
            pltpu.VMEM((stacked, KEYS), jnp.bfloat16),
            pltpu.VMEM((stacked, KEYS), jnp.bfloat16),
        ],
        compiler_params=pltpu.CompilerParams(vmem_limit_bytes=48 * 2**20),
        cost_estimate=pl.CostEstimate(
            flops=12 * CHIP * KEYS * HD * GROUPS * HEADS,
            bytes_accessed=8 * 2**20,
            transcendentals=CHIP * KEYS * GROUPS * HEADS,
        ),
        name="attention",
    )(starts, q, qt, u, ut, far, near, here)


def projection_kernel(
    place_ref, mine_ref, other_ref, own_ref, left_ref, right_ref, far_ref, out_ref, tokens, weight, sems
):
    core, a = place_ref[0], place_ref[1]
    pieces = ((own_ref, 0), (left_ref, 3), (right_ref, 1), (far_ref, 2))

    def copies(z):
        return [
            pltpu.make_async_copy(
                ref.at[:, z], weight.at[z, pl.ds(lax.rem(a + turn, 4) * 4, 4)], sems.at[z, i]
            )
            for i, (ref, turn) in enumerate(pieces)
        ]

    for z in range(SHARDS):
        for copy in copies(z):
            copy.start()
    mine = pl.multiple_of(core * BLOCK, BLOCK)
    tokens[pl.ds(mine, BLOCK), :] = mine_ref[...]
    tokens[pl.ds(BLOCK - mine, BLOCK), :] = other_ref[...]
    total = jnp.zeros(out_ref.shape, jnp.float32)
    for z in range(SHARDS):
        for copy in copies(z):
            copy.wait()
        depth = SLICES * ROWS
        total += jnp.dot(
            tokens[:, z * depth : (z + 1) * depth],
            weight[z].reshape(depth, out_ref.shape[1]),
            preferred_element_type=jnp.float32,
        )
    out_ref[...] = total.astype(out_ref.dtype)


def projection(place, mine, other, own, left, right, far):
    width = own.shape[-1]
    depth = mine.shape[1]
    vmem = pl.BlockSpec(memory_space=pltpu.VMEM)
    away = pl.BlockSpec(memory_space=pl.ANY)
    return pl.pallas_call(
        projection_kernel,
        in_specs=[pl.BlockSpec(memory_space=pltpu.SMEM), vmem, vmem, away, away, away, away],
        out_specs=vmem,
        out_shape=jax.ShapeDtypeStruct((CHIP, width), jnp.bfloat16),
        scratch_shapes=[
            pltpu.VMEM((CHIP, depth), jnp.bfloat16),
            pltpu.VMEM((SHARDS, SLICES, ROWS, width), jnp.bfloat16),
            pltpu.SemaphoreType.DMA((SHARDS, 4)),
        ],
        compiler_params=pltpu.CompilerParams(vmem_limit_bytes=32 * 2**20),
        cost_estimate=pl.CostEstimate(
            flops=2 * CHIP * depth * width, bytes_accessed=6 * 2**20, transcendentals=0
        ),
        name="projection",
    )(place, mine, other, own, left, right, far)


def ring_of(core, x, y, turn, first):
    if (core == 0) == first:
        return x, (y + turn) % 4
    return (x + turn) % 4, y


def number(x, y, core):
    return (x * 4 + y) * CORES + core


def in_plane():
    return [(x, y, core) for x in range(4) for y in range(4) for core in range(CORES)]


def gathered(rows, device):
    chip, core = device // CORES, device % CORES
    x, y = chip // 4, chip % 4
    a, b = jnp.where(core == 0, x, y), jnp.where(core == 0, y, x)
    piece = lax.dynamic_slice_in_dim(rows, (a * 4 + b) * ROWS, ROWS, 0)
    piece = jnp.broadcast_to(piece[None], (SHARDS,) + piece.shape)
    piece = lax.all_to_all(piece, "fsdp", 0, 0)
    groups = {}
    for place in in_plane():
        members = [number(*ring_of(place[2], *place[:2], turn, True), place[2]) for turn in range(4)]
        groups[tuple(sorted(members))] = None
    piece = jnp.broadcast_to(piece[None], (4,) + piece.shape)
    own = lax.all_to_all(piece, "tok", 0, 0, axis_index_groups=[list(g) for g in groups])

    def turned(turn):
        route = [
            (number(*place), number(*ring_of(place[2], *place[:2], turn, False), place[2]))
            for place in in_plane()
        ]
        return lax.ppermute(own, "tok", route)

    return a, own, turned(1), turned(-1), turned(2)


def body(hidden, queries, upstream, context_weight, lengths):
    device = lax.axis_index("tok")
    core, chip = device % CORES, device // CORES
    ordered = context_weight.reshape(-1, 2, CORES, GROUPS, HD)
    ordered = lax.dynamic_slice_in_dim(ordered, core, 1, 2)[:, :, 0]
    ordered = ordered.transpose(0, 2, 1, 3).reshape(-1, GROUPS * 2 * HD)
    a, own, left, right, opposite = gathered(ordered, device)

    hidden, queries, upstream, _ = lax.optimization_barrier((hidden, queries, upstream, own))
    other_hidden = swapped(hidden)

    def heads_of(block):
        mine = half(block, core, 1)
        other = swapped(half(block, 1 - core, 1))
        whole = by_core(core, mine, other, 0).reshape(CORES, BLOCK, GROUPS, HEADS, HD)
        rows = whole.transpose(0, 2, 3, 1, 4).reshape(CORES, GROUPS, HEADS * BLOCK, HD)
        columns = whole.transpose(0, 2, 4, 3, 1).reshape(CORES, GROUPS, HD, HEADS * BLOCK)
        return rows, columns

    q, qt = heads_of(queries)
    u, ut = heads_of(upstream)
    bounds = jnp.cumsum(lengths[0])
    places = chip * CHIP + jnp.arange(CHIP, dtype=jnp.int32)
    starts = jnp.max(jnp.where(bounds[None, :] <= places[:, None], bounds[None, :], 0), axis=1)
    starts = (starts - chip * CHIP).astype(jnp.int32)[:, None]
    place = jnp.stack([core, a]).astype(jnp.int32)
    place, q, qt, u, ut, starts, opposite = lax.optimization_barrier(
        (place, q, qt, u, ut, starts, opposite)
    )

    here = projection(place, hidden, other_hidden, own, left, right, opposite)
    near = shifted(here, CORES)
    far = shifted(here, 2 * CORES)
    logs, dq, dfar, dnear, dhere = attention(starts, q, qt, u, ut, far, near, here)

    context_slopes = (
        dhere
        + shifted(dnear, -CORES).astype(jnp.float32)
        + shifted(dfar, -2 * CORES).astype(jnp.float32)
    ).astype(jnp.bfloat16)
    query_slopes = by_core(core, half(dq, core, 0), swapped(half(dq, 1 - core, 0)), 1)
    log_totals = by_core(core, half(logs, core, 0)[0], swapped(half(logs, 1 - core, 0)[0]), 0)
    context_slopes = by_core(
        core, half(context_slopes, core, 0), swapped(half(context_slopes, 1 - core, 0)), 1
    )
    context_slopes = context_slopes.reshape(BLOCK, KVH, 2, HD).transpose(0, 2, 1, 3)
    return log_totals, query_slopes, context_slopes.reshape(BLOCK, 2 * KVH * HD)


def solution(mesh):
    in_specs = (
        P(("fsdp", "tok"), None),
        P(("fsdp", "tok"), None),
        P(("fsdp", "tok"), None),
        P("fsdp", None),
        P("fsdp", None),
    )
    out_specs = (P(None, ("fsdp", "tok")), P(("fsdp", "tok"), None), P(("fsdp", "tok"), None))
    return jax.shard_map(body, mesh=mesh, in_specs=in_specs, out_specs=out_specs, check_vma=False)
```

```python
import functools
import math

import jax
import jax.numpy as jnp
from jax import lax
from jax.experimental import pallas as pl
from jax.experimental.pallas import tpu as pltpu
from jax.sharding import PartitionSpec as P

QH = 32
KVH = 4
HD = 128
CORES = 2
BLOCK = 128
CHIP = CORES * BLOCK
GROUPS = KVH // CORES
HEADS = QH // KVH
DOCS = 16
LENGTHS = 3
SPAN = 4 * BLOCK
KEYS = SPAN + BLOCK
SHARDS = 16
SLICES = 16
ROWS = 16
SCALE = 1.0 / math.sqrt(HD)
LOG2E = math.log2(math.e)


def shifted(block, distance, across=False):
    count = lax.axis_size("tok")
    route = [(i, i + distance) for i in range(count) if 0 <= i + distance < count]
    if across:
        route = [(i, j ^ 1) for i, j in route]
    return lax.ppermute(block, "tok", route)


def swapped(block):
    count = lax.axis_size("tok")
    return lax.ppermute(block, "tok", [(i, i ^ 1) for i in range(count)])


def half(block, index, axis):
    size = block.shape[axis] // 2
    return lax.dynamic_slice_in_dim(block, index * size, size, axis)


def attention_kernel(
    place_ref, q_mine, q_other, u_mine, u_other, far_ref, near_ref, here_ref,
    log_mine, dq_mine, to_core, here_mine, near_mine, near_other, far_mine, far_other,
    keys, values, sums, bias, q_rows, u_rows, weight_rows, change_rows,
):
    group, part = pl.program_id(0), pl.program_id(1)
    core, chip = place_ref[0], place_ref[1]
    first = pl.multiple_of(jnp.where(part == 0, core, 1 - core) * BLOCK, BLOCK)

    def stack(q_ref, u_ref):
        for head in range(HEADS):
            rows, columns = slice(head * BLOCK, (head + 1) * BLOCK), slice(head * HD, (head + 1) * HD)
            q_rows[rows, :] = q_ref[:, columns]
            u_rows[rows, :] = u_ref[:, columns]

    @pl.when(part == 0)
    def _():
        for i, ref in enumerate((far_ref, near_ref, here_ref)):
            keys[i * CHIP : (i + 1) * CHIP, :] = ref[:, :HD]
            values[i * CHIP : (i + 1) * CHIP, :] = ref[:, HD:]
        sums[...] = jnp.zeros_like(sums)
        stack(q_mine, u_mine)

    @pl.when(part == 1)
    def _():
        stack(q_other, u_other)

    key_window = keys[pl.ds(first, KEYS), :]
    value_window = values[pl.ds(first, KEYS), :]
    places = first - SPAN + lax.broadcasted_iota(jnp.int32, (BLOCK, KEYS), 1)
    own = first + lax.broadcasted_iota(jnp.int32, (BLOCK, KEYS), 0)
    token = first + lax.broadcasted_iota(jnp.int32, (BLOCK, 1), 0)
    start, bound = jnp.zeros((BLOCK, 1), jnp.int32) - chip * CHIP, -chip * CHIP
    for i in range(DOCS):
        bound = bound + place_ref[LENGTHS + i]
        start = jnp.where(token >= bound, bound, start)
    bias[...] = jnp.where((places <= own) & (places >= start), 0.0, -jnp.inf)
    over_rows = (((1,), (1,)), ((), ()))
    dot = functools.partial(jnp.dot, preferred_element_type=jnp.float32)
    dot_rows = functools.partial(
        lax.dot_general, dimension_numbers=over_rows, preferred_element_type=jnp.float32
    )
    count = HEADS // 2
    stripes = [slice(i * count * BLOCK, (i + 1) * count * BLOCK) for i in range(2)]
    scores = [dot_rows(q_rows[rows, :], key_window) for rows in stripes]
    pushed = [dot_rows(u_rows[rows, :], value_window) for rows in stripes]
    weights, logs, attended = [], [], []
    for i, rows in enumerate(stripes):
        masked = scores[i].reshape(count, BLOCK, KEYS) + bias[...][None]
        masked = masked.reshape(count * BLOCK, KEYS)
        highest = jnp.max(masked, axis=1, keepdims=True)
        raised = jnp.exp2((masked - highest) * (SCALE * LOG2E))
        total = jnp.sum(raised, axis=1, keepdims=True)
        logs.append(highest * SCALE + jnp.log(total))
        weights.append(raised * (1.0 / total))
        weight_rows[rows, :] = weights[i].astype(jnp.bfloat16)
        attended.append(dot(weights[i].astype(jnp.bfloat16), value_window).astype(jnp.bfloat16))
    value_slope, key_slope = [], []
    for i, rows in enumerate(stripes):
        product = u_rows[rows, :].astype(jnp.float32) * attended[i].astype(jnp.float32)
        inner = jnp.sum(product, axis=1, keepdims=True)
        change_rows[rows, :] = (weights[i] * (pushed[i] - inner)).astype(jnp.bfloat16)
        value_slope.append(dot(u_rows[rows, :].T, weight_rows[rows, :]))
    slopes = [dot(change_rows[rows, :], key_window) * SCALE for rows in stripes]
    for rows in stripes:
        key_slope.append(dot(q_rows[rows, :].T, change_rows[rows, :]))
    sums[pl.ds(first, KEYS), :HD] += (key_slope[0] + key_slope[1]).T * SCALE
    sums[pl.ds(first, KEYS), HD:] += (value_slope[0] + value_slope[1]).T
    lane = lax.broadcasted_iota(jnp.int32, (BLOCK, HD), 1)
    columns = jnp.zeros((BLOCK, HD), jnp.float32)
    for head in range(HEADS):
        rows = slice(head % count * BLOCK, (head % count + 1) * BLOCK)
        columns = jnp.where(lane % HEADS == head, logs[head // count][rows], columns)

    def head_slope(head):
        rows = slice(head % count * BLOCK, (head % count + 1) * BLOCK)
        return slopes[head // count][rows].astype(jnp.bfloat16)

    @pl.when(part == 0)
    def _():
        log_mine[...] = columns.T[:HEADS]
        for head in range(HEADS):
            dq_mine[:, head * HD : (head + 1) * HD] = head_slope(head)

    @pl.when(part == 1)
    def _():
        high = columns.astype(jnp.bfloat16).astype(jnp.float32)
        middle = (columns - high).astype(jnp.bfloat16).astype(jnp.float32)
        terms = jnp.where(lane < HEADS, high, jnp.where(lane < 2 * HEADS, middle, columns - high - middle))
        mine = pl.multiple_of(core * BLOCK, BLOCK)
        others = pl.multiple_of(BLOCK - mine, BLOCK)

        def rows_of(first, which):
            return sums[pl.ds(first + which, BLOCK), :]

        here_mine[...] = rows_of(SPAN, mine)
        near_mine[...] = rows_of(CHIP, mine).astype(jnp.bfloat16)
        near_other[...] = rows_of(CHIP, others).astype(jnp.bfloat16)
        far_mine[...] = rows_of(0, mine).astype(jnp.bfloat16)
        far_other[...] = rows_of(0, others).astype(jnp.bfloat16)
        here_other = rows_of(SPAN, others).astype(jnp.bfloat16)
        for g in range(GROUPS):

            @pl.when(group == g)
            def _():
                for head in range(HEADS):
                    at = (g * HEADS + head) * HD
                    to_core[:, at : at + HD] = head_slope(head)
                at = GROUPS * HEADS * HD + g * 3 * HD
                to_core[:, at : at + 2 * HD] = here_other
                to_core[:, at + 2 * HD : at + 3 * HD] = terms.astype(jnp.bfloat16)


def attention(place, queries, q_other, upstream, u_other, far, near, here):
    stacked = HEADS * BLOCK
    mine = pl.BlockSpec((BLOCK, HEADS * HD), lambda g, b, place: (0, place[0] * GROUPS + g))
    other = pl.BlockSpec((BLOCK, HEADS * HD), lambda g, b, place: (0, g))
    context = pl.BlockSpec((CHIP, 2 * HD), lambda g, b, place: (0, g))
    block = pl.BlockSpec((BLOCK, 2 * HD), lambda g, b, place: (0, g))
    log = pl.BlockSpec((HEADS, BLOCK), lambda g, b, place: (g, 0))
    wide, packed, heads = GROUPS * 2 * HD, GROUPS * 3 * HD, GROUPS * HEADS
    term = jax.ShapeDtypeStruct((BLOCK, wide), jnp.bfloat16)
    return pl.pallas_call(
        attention_kernel,
        grid_spec=pltpu.PrefetchScalarGridSpec(
            num_scalar_prefetch=1,
            grid=(GROUPS, CORES),
            in_specs=[
                mine, other, mine, other, context, context, context,
            ],
            out_specs=[
                log, other,
                pl.BlockSpec((BLOCK, heads * HD + packed), lambda g, b, place: (0, 0)),
                block, block, block, block, block,
            ],
            scratch_shapes=[
                pltpu.VMEM((SPAN + CHIP, HD), jnp.bfloat16),
                pltpu.VMEM((SPAN + CHIP, HD), jnp.bfloat16),
                pltpu.VMEM((SPAN + CHIP, 2 * HD), jnp.float32),
                pltpu.VMEM((BLOCK, KEYS), jnp.float32),
                pltpu.VMEM((stacked, HD), jnp.bfloat16),
                pltpu.VMEM((stacked, HD), jnp.bfloat16),
                pltpu.VMEM((stacked, KEYS), jnp.bfloat16),
                pltpu.VMEM((stacked, KEYS), jnp.bfloat16),
            ],
        ),
        out_shape=[
            jax.ShapeDtypeStruct((heads, BLOCK), jnp.float32),
            jax.ShapeDtypeStruct((BLOCK, heads * HD), jnp.bfloat16),
            jax.ShapeDtypeStruct((BLOCK, heads * HD + packed), jnp.bfloat16),
            jax.ShapeDtypeStruct((BLOCK, wide), jnp.float32),
            term, term, term, term,
        ],
        compiler_params=pltpu.CompilerParams(vmem_limit_bytes=48 * 2**20),
        cost_estimate=pl.CostEstimate(
            flops=12 * CHIP * KEYS * HD * GROUPS * HEADS,
            bytes_accessed=8 * 2**20,
            transcendentals=CHIP * KEYS * GROUPS * HEADS,
        ),
        name="attention",
    )(place, queries, q_other, upstream, u_other, far, near, here)


def finish_kernel(
    place_ref, dq_mine, from_core, log_mine, here_mine, near_mine, far_mine, near_other, far_other,
    log_ref, dq_ref, context_ref,
):
    width, heads = dq_mine.shape[1], log_mine.shape[0]

    def put(which, dq, log, slopes):
        dq_ref[:, which * width : (which + 1) * width] = dq
        for g in range(GROUPS):
            row = which * heads + g * HEADS
            log_ref[row : row + HEADS, :] = log[g]
            for kind in range(2):
                to = (kind * KVH + which * GROUPS + g) * HD
                context_ref[:, to : to + HD] = slopes[g][:, kind * HD : (kind + 1) * HD]

    def total(here, near, far, g):
        at = slice(g * 2 * HD, (g + 1) * 2 * HD)
        terms = here + near[:, at].astype(jnp.float32) + far[:, at].astype(jnp.float32)
        return terms.astype(jnp.bfloat16)

    mine, other, logs = [], [], []
    for g in range(GROUPS):
        at = width + g * 3 * HD
        mine.append(total(here_mine[:, g * 2 * HD : (g + 1) * 2 * HD], near_mine, far_mine, g))
        here = from_core[:, at : at + 2 * HD].astype(jnp.float32)
        other.append(total(here, near_other, far_other, g))
        terms = from_core[:, at + 2 * HD : at + 3 * HD].astype(jnp.float32).T
        logs.append(terms[:HEADS] + terms[HEADS : 2 * HEADS] + terms[2 * HEADS : 3 * HEADS])
    own_logs = [log_mine[g * HEADS : (g + 1) * HEADS, :] for g in range(GROUPS)]
    for core in range(CORES):

        @pl.when(place_ref[0] == core)
        def _():
            put(core, dq_mine[...], own_logs, mine)
            put(1 - core, from_core[:, :width], logs, other)


def finish(place, *terms):
    vmem = pl.BlockSpec(memory_space=pltpu.VMEM)
    return pl.pallas_call(
        finish_kernel,
        in_specs=[pl.BlockSpec(memory_space=pltpu.SMEM)] + [vmem] * len(terms),
        out_specs=[vmem] * 3,
        out_shape=[
            jax.ShapeDtypeStruct((QH, BLOCK), jnp.float32),
            jax.ShapeDtypeStruct((BLOCK, QH * HD), jnp.bfloat16),
            jax.ShapeDtypeStruct((BLOCK, 2 * KVH * HD), jnp.bfloat16),
        ],
        compiler_params=pltpu.CompilerParams(vmem_limit_bytes=32 * 2**20),
        cost_estimate=pl.CostEstimate(flops=0, bytes_accessed=4 * 2**20, transcendentals=0),
        name="finish",
    )(place, *terms)


def projection_kernel(
    place_ref, mine_ref, other_ref, own_ref, left_ref, right_ref, far_ref, out_ref, tokens, weight, sems
):
    core, a = place_ref[0], place_ref[2]
    pieces = ((own_ref, 0), (left_ref, 3), (right_ref, 1), (far_ref, 2))

    copies = [
        pltpu.make_async_copy(
            ref.at[b], weight.at[lax.rem(a + turn, 4) * 4 + b], sems.at[i, b]
        )
        for i, (ref, turn) in enumerate(pieces)
        for b in range(4)
    ]
    for copy in copies:
        copy.start()
    mine = pl.multiple_of(core * BLOCK, BLOCK)
    tokens[pl.ds(mine, BLOCK), :] = mine_ref[...]
    tokens[pl.ds(BLOCK - mine, BLOCK), :] = other_ref[...]
    for copy in copies:
        copy.wait()
    total = jnp.zeros(out_ref.shape, jnp.float32)
    depth = SLICES * ROWS
    for z in range(SHARDS):
        total += jnp.dot(
            tokens[:, z * depth : (z + 1) * depth],
            weight[:, z].reshape(depth, out_ref.shape[1]),
            preferred_element_type=jnp.float32,
        )
    out_ref[...] = total.astype(out_ref.dtype)


def projection(place, mine, other, own, left, right, far):
    width = own.shape[-1]
    depth = mine.shape[1]
    vmem = pl.BlockSpec(memory_space=pltpu.VMEM)
    away = pl.BlockSpec(memory_space=pl.ANY)
    return pl.pallas_call(
        projection_kernel,
        in_specs=[pl.BlockSpec(memory_space=pltpu.SMEM), vmem, vmem, away, away, away, away],
        out_specs=vmem,
        out_shape=jax.ShapeDtypeStruct((CHIP, width), jnp.bfloat16),
        scratch_shapes=[
            pltpu.VMEM((CHIP, depth), jnp.bfloat16),
            pltpu.VMEM((SLICES, SHARDS, ROWS, width), jnp.bfloat16),
            pltpu.SemaphoreType.DMA((4, 4)),
        ],
        compiler_params=pltpu.CompilerParams(vmem_limit_bytes=32 * 2**20),
        cost_estimate=pl.CostEstimate(
            flops=2 * CHIP * depth * width, bytes_accessed=6 * 2**20, transcendentals=0
        ),
        name="projection",
    )(place, mine, other, own, left, right, far)


def ring_of(core, x, y, turn, first):
    if (core == 0) == first:
        return x, (y + turn) % 4
    return (x + turn) % 4, y


def number(x, y, core):
    return (x * 4 + y) * CORES + core


def in_plane():
    return [(x, y, core) for x in range(4) for y in range(4) for core in range(CORES)]


def gathered(rows, device):
    chip, core = device // CORES, device % CORES
    x, y = chip // 4, chip % 4
    a, b = jnp.where(core == 0, x, y), jnp.where(core == 0, y, x)
    piece = lax.dynamic_slice_in_dim(rows, (a * 4 + b) * ROWS, ROWS, 0)
    piece = jnp.broadcast_to(piece[None], (SHARDS,) + piece.shape)
    piece = lax.all_to_all(piece, "fsdp", 0, 0)
    groups = {}
    for place in in_plane():
        members = [number(*ring_of(place[2], *place[:2], turn, True), place[2]) for turn in range(4)]
        groups[tuple(sorted(members))] = None
    piece = jnp.broadcast_to(piece[None], (4,) + piece.shape)
    own = lax.all_to_all(piece, "tok", 0, 0, axis_index_groups=[list(g) for g in groups])

    def turned(turn):
        route = [
            (number(*place), number(*ring_of(place[2], *place[:2], turn, False), place[2]))
            for place in in_plane()
        ]
        return lax.ppermute(own, "tok", route)

    return a, own, turned(1), turned(-1), turned(2)


def body(hidden, queries, upstream, context_weight, lengths):
    device = lax.axis_index("tok")
    core, chip = device % CORES, device // CORES
    ordered = context_weight.reshape(-1, 2, CORES, GROUPS, HD)
    ordered = lax.dynamic_slice_in_dim(ordered, core, 1, 2)[:, :, 0]
    ordered = ordered.transpose(0, 2, 1, 3).reshape(-1, GROUPS * 2 * HD)
    a, own, left, right, opposite = gathered(ordered, device)

    hidden, queries, upstream, _ = lax.optimization_barrier((hidden, queries, upstream, own))
    other_hidden = swapped(hidden)
    q_other = swapped(half(queries, 1 - core, 1))
    u_other = swapped(half(upstream, 1 - core, 1))
    place = jnp.concatenate([jnp.stack([core, chip, a]).astype(jnp.int32), lengths[0]])
    place, q_other, u_other, opposite = lax.optimization_barrier((place, q_other, u_other, opposite))

    here = projection(place, hidden, other_hidden, own, left, right, opposite)
    near = shifted(here, CORES)
    far = shifted(here, 2 * CORES)
    (
        log_mine, dq_mine, to_core, here_mine, near_mine, near_other, far_mine, far_other,
    ) = attention(place, queries, q_other, upstream, u_other, far, near, here)
    far_mine, far_other = shifted(far_mine, -2 * CORES), shifted(far_other, -2 * CORES, True)
    near_mine, near_other = shifted(near_mine, -CORES), shifted(near_other, -CORES, True)
    from_core = swapped(to_core)
    return tuple(
        finish(
            place, dq_mine, from_core, log_mine, here_mine, near_mine, far_mine, near_other, far_other
        )
    )


def solution(mesh):
    in_specs = (
        P(("fsdp", "tok"), None),
        P(("fsdp", "tok"), None),
        P(("fsdp", "tok"), None),
        P("fsdp", None),
        P("fsdp", None),
    )
    out_specs = (P(None, ("fsdp", "tok")), P(("fsdp", "tok"), None), P(("fsdp", "tok"), None))
    return jax.shard_map(body, mesh=mesh, in_specs=in_specs, out_specs=out_specs, check_vma=False)
```

```python
import functools
import math

import jax
import jax.numpy as jnp
from jax import lax
from jax.experimental import pallas as pl
from jax.experimental.pallas import tpu as pltpu
from jax.sharding import PartitionSpec as P

QH = 32
KVH = 4
HD = 128
CORES = 2
BLOCK = 128
CHIP = CORES * BLOCK
GROUPS = KVH // CORES
HEADS = QH // KVH
DOCS = 16
KINDS = 3
LENGTHS = 6
SPAN = 4 * BLOCK
CHIPS = 2
KEYS = SPAN + BLOCK
SHARDS = 16
SLICES = 8
ROWS = 32
SCALE = 1.0 / math.sqrt(HD)
LOG2E = math.log2(math.e)


def shifted(block, distance, across=False):
    count = lax.axis_size("tok")
    route = [(i, i + distance) for i in range(count) if 0 <= i + distance < count]
    if across:
        route = [(i, j ^ 1) for i, j in route]
    return lax.ppermute(block, "tok", route)


def partner(device):
    return device ^ (2 if device % CORES else 8)


def paired(block, distance=0, across=False):
    count = lax.axis_size("tok")
    route = [(partner(i) ^ (1 if across else 0), i) for i in range(count)]
    route = [(i, j + distance) for i, j in route if j + distance < count]
    return lax.ppermute(block, "tok", route)


def swapped(block):
    count = lax.axis_size("tok")
    return lax.ppermute(block, "tok", [(i, i ^ 1) for i in range(count)])


def half(block, index, axis):
    size = block.shape[axis] // 2
    return lax.dynamic_slice_in_dim(block, index * size, size, axis)


def attention_kernel(
    place_ref, q_mine, q_other, u_mine, u_other, *refs
):
    group, part = pl.program_id(0), pl.program_id(1)
    core, chip = place_ref[0], place_ref[1]
    window, refs = refs[:6], refs[6:]
    log_mine, dq_mine, to_core, here_mine, near_mine, near_other, far_mine, far_other = refs[:8]
    keys, values, sums, bias, q_rows, u_rows, weight_rows, change_rows = refs[8:]
    first = pl.multiple_of(jnp.where(part == 0, core, 1 - core) * BLOCK, BLOCK)

    def stack(q_ref, u_ref):
        for head in range(HEADS):
            rows, columns = slice(head * BLOCK, (head + 1) * BLOCK), slice(head * HD, (head + 1) * HD)
            q_rows[rows, :] = q_ref[:, columns]
            u_rows[rows, :] = u_ref[:, columns]

    @pl.when(part == 0)
    def _():
        for i in range(3):
            rows = slice(i * CHIP, (i + 1) * CHIP)
            for kind in range(GROUPS):

                @pl.when((place_ref[KINDS + 2 - i] == group) == (kind == 0))
                def _():
                    keys[rows, :] = window[2 * i + kind][:, :HD]
                    values[rows, :] = window[2 * i + kind][:, HD:]

        sums[...] = jnp.zeros_like(sums)
        stack(q_mine, u_mine)

    @pl.when(part == 1)
    def _():
        stack(q_other, u_other)

    key_window = keys[pl.ds(first, KEYS), :]
    value_window = values[pl.ds(first, KEYS), :]
    places = first - SPAN + lax.broadcasted_iota(jnp.int32, (BLOCK, KEYS), 1)
    own = first + lax.broadcasted_iota(jnp.int32, (BLOCK, KEYS), 0)
    token = first + lax.broadcasted_iota(jnp.int32, (BLOCK, 1), 0)
    start, bound = jnp.zeros((BLOCK, 1), jnp.int32) - chip * CHIP, -chip * CHIP
    for i in range(DOCS):
        bound = bound + place_ref[LENGTHS + i]
        start = jnp.where(token >= bound, bound, start)
    bias[...] = jnp.where((places <= own) & (places >= start), 0.0, -jnp.inf)
    over_rows = (((1,), (1,)), ((), ()))
    dot = functools.partial(jnp.dot, preferred_element_type=jnp.float32)
    dot_rows = functools.partial(
        lax.dot_general, dimension_numbers=over_rows, preferred_element_type=jnp.float32
    )
    count = HEADS // 2
    stripes = [slice(i * count * BLOCK, (i + 1) * count * BLOCK) for i in range(2)]
    scores = [dot_rows(q_rows[rows, :], key_window) for rows in stripes]
    pushed = [dot_rows(u_rows[rows, :], value_window) for rows in stripes]
    weights, logs, attended = [], [], []
    for i, rows in enumerate(stripes):
        masked = scores[i].reshape(count, BLOCK, KEYS) + bias[...][None]
        masked = masked.reshape(count * BLOCK, KEYS)
        highest = jnp.max(masked, axis=1, keepdims=True)
        raised = jnp.exp2((masked - highest) * (SCALE * LOG2E))
        total = jnp.sum(raised, axis=1, keepdims=True)
        logs.append(highest * SCALE + jnp.log(total))
        weights.append(raised * (1.0 / total))
        weight_rows[rows, :] = weights[i].astype(jnp.bfloat16)
        attended.append(dot(weights[i].astype(jnp.bfloat16), value_window).astype(jnp.bfloat16))
    value_slope, key_slope = [], []
    for i, rows in enumerate(stripes):
        product = u_rows[rows, :].astype(jnp.float32) * attended[i].astype(jnp.float32)
        inner = jnp.sum(product, axis=1, keepdims=True)
        change_rows[rows, :] = (weights[i] * (pushed[i] - inner)).astype(jnp.bfloat16)
        value_slope.append(dot(u_rows[rows, :].T, weight_rows[rows, :]))
    slopes = [dot(change_rows[rows, :], key_window) * SCALE for rows in stripes]
    for rows in stripes:
        key_slope.append(dot(q_rows[rows, :].T, change_rows[rows, :]))
    sums[pl.ds(first, KEYS), :HD] += (key_slope[0] + key_slope[1]).T * SCALE
    sums[pl.ds(first, KEYS), HD:] += (value_slope[0] + value_slope[1]).T
    lane = lax.broadcasted_iota(jnp.int32, (BLOCK, HD), 1)
    columns = jnp.zeros((BLOCK, HD), jnp.float32)
    for head in range(HEADS):
        rows = slice(head % count * BLOCK, (head % count + 1) * BLOCK)
        columns = jnp.where(lane % HEADS == head, logs[head // count][rows], columns)

    def head_slope(head):
        rows = slice(head % count * BLOCK, (head % count + 1) * BLOCK)
        return slopes[head // count][rows].astype(jnp.bfloat16)

    @pl.when(part == 0)
    def _():
        log_mine[...] = columns.T[:HEADS]
        for head in range(HEADS):
            dq_mine[:, head * HD : (head + 1) * HD] = head_slope(head)

    @pl.when(part == 1)
    def _():
        high = columns.astype(jnp.bfloat16).astype(jnp.float32)
        middle = (columns - high).astype(jnp.bfloat16).astype(jnp.float32)
        terms = jnp.where(lane < HEADS, high, jnp.where(lane < 2 * HEADS, middle, columns - high - middle))
        mine = pl.multiple_of(core * BLOCK, BLOCK)
        others = pl.multiple_of(BLOCK - mine, BLOCK)

        def rows_of(first, which):
            return sums[pl.ds(first + which, BLOCK), :]

        here_mine[...] = rows_of(SPAN, mine)
        near_mine[...] = rows_of(CHIP, mine).astype(jnp.bfloat16)
        near_other[...] = rows_of(CHIP, others).astype(jnp.bfloat16)
        far_mine[...] = rows_of(0, mine).astype(jnp.bfloat16)
        far_other[...] = rows_of(0, others).astype(jnp.bfloat16)
        here_other = rows_of(SPAN, others).astype(jnp.bfloat16)
        for g in range(GROUPS):

            @pl.when(group == g)
            def _():
                for head in range(HEADS):
                    at = (g * HEADS + head) * HD
                    to_core[:, at : at + HD] = head_slope(head)
                at = GROUPS * HEADS * HD + g * 3 * HD
                to_core[:, at : at + 2 * HD] = here_other
                to_core[:, at + 2 * HD : at + 3 * HD] = terms.astype(jnp.bfloat16)


def attention(place, queries, q_other, upstream, u_other, *window):
    stacked = HEADS * BLOCK
    mine = pl.BlockSpec((BLOCK, HEADS * HD), lambda g, b, place: (0, place[0] * GROUPS + g))
    other = pl.BlockSpec((BLOCK, HEADS * HD), lambda g, b, place: (0, g))
    context = pl.BlockSpec((CHIP, 2 * HD), lambda g, b, place: (0, 0))
    block = pl.BlockSpec((BLOCK, 2 * HD), lambda g, b, place: (0, g))
    log = pl.BlockSpec((HEADS, BLOCK), lambda g, b, place: (g, 0))
    wide, packed, heads = GROUPS * 2 * HD, GROUPS * 3 * HD, GROUPS * HEADS
    term = jax.ShapeDtypeStruct((BLOCK, wide), jnp.bfloat16)
    return pl.pallas_call(
        attention_kernel,
        grid_spec=pltpu.PrefetchScalarGridSpec(
            num_scalar_prefetch=1,
            grid=(GROUPS, CORES),
            in_specs=[
                mine, other, mine, other, *[context] * 6,
            ],
            out_specs=[
                log, other,
                pl.BlockSpec((BLOCK, heads * HD + packed), lambda g, b, place: (0, 0)),
                block, block, block, block, block,
            ],
            scratch_shapes=[
                pltpu.VMEM((SPAN + CHIP, HD), jnp.bfloat16),
                pltpu.VMEM((SPAN + CHIP, HD), jnp.bfloat16),
                pltpu.VMEM((SPAN + CHIP, 2 * HD), jnp.float32),
                pltpu.VMEM((BLOCK, KEYS), jnp.float32),
                pltpu.VMEM((stacked, HD), jnp.bfloat16),
                pltpu.VMEM((stacked, HD), jnp.bfloat16),
                pltpu.VMEM((stacked, KEYS), jnp.bfloat16),
                pltpu.VMEM((stacked, KEYS), jnp.bfloat16),
            ],
        ),
        out_shape=[
            jax.ShapeDtypeStruct((heads, BLOCK), jnp.float32),
            jax.ShapeDtypeStruct((BLOCK, heads * HD), jnp.bfloat16),
            jax.ShapeDtypeStruct((BLOCK, heads * HD + packed), jnp.bfloat16),
            jax.ShapeDtypeStruct((BLOCK, wide), jnp.float32),
            term, term, term, term,
        ],
        compiler_params=pltpu.CompilerParams(vmem_limit_bytes=48 * 2**20),
        cost_estimate=pl.CostEstimate(
            flops=12 * CHIP * KEYS * HD * GROUPS * HEADS,
            bytes_accessed=8 * 2**20,
            transcendentals=CHIP * KEYS * GROUPS * HEADS,
        ),
        name="attention",
    )(place, queries, q_other, upstream, u_other, *window)


def finish_kernel(
    place_ref, dq_mine, from_core, log_mine, here_mine, near_mine, far_mine, near_other, far_other,
    log_ref, dq_ref, context_ref,
):
    width, heads = dq_mine.shape[1], log_mine.shape[0]

    def put(which, dq, log, slopes):
        dq_ref[:, which * width : (which + 1) * width] = dq
        for g in range(GROUPS):
            row = which * heads + g * HEADS
            log_ref[row : row + HEADS, :] = log[g]
            for kind in range(2):
                to = (kind * KVH + which * GROUPS + g) * HD
                context_ref[:, to : to + HD] = slopes[g][:, kind * HD : (kind + 1) * HD]

    def total(here, near, far, g):
        at = slice(g * 2 * HD, (g + 1) * 2 * HD)
        terms = here + near[:, at].astype(jnp.float32) + far[:, at].astype(jnp.float32)
        return terms.astype(jnp.bfloat16)

    mine, other, logs = [], [], []
    for g in range(GROUPS):
        at = width + g * 3 * HD
        mine.append(total(here_mine[:, g * 2 * HD : (g + 1) * 2 * HD], near_mine, far_mine, g))
        here = from_core[:, at : at + 2 * HD].astype(jnp.float32)
        other.append(total(here, near_other, far_other, g))
        terms = from_core[:, at + 2 * HD : at + 3 * HD].astype(jnp.float32).T
        logs.append(terms[:HEADS] + terms[HEADS : 2 * HEADS] + terms[2 * HEADS : 3 * HEADS])
    own_logs = [log_mine[g * HEADS : (g + 1) * HEADS, :] for g in range(GROUPS)]
    for core in range(CORES):

        @pl.when(place_ref[0] == core)
        def _():
            put(core, dq_mine[...], own_logs, mine)
            put(1 - core, from_core[:, :width], logs, other)


def finish(place, *terms):
    vmem = pl.BlockSpec(memory_space=pltpu.VMEM)
    return pl.pallas_call(
        finish_kernel,
        in_specs=[pl.BlockSpec(memory_space=pltpu.SMEM)] + [vmem] * len(terms),
        out_specs=[vmem] * 3,
        out_shape=[
            jax.ShapeDtypeStruct((QH, BLOCK), jnp.float32),
            jax.ShapeDtypeStruct((BLOCK, QH * HD), jnp.bfloat16),
            jax.ShapeDtypeStruct((BLOCK, 2 * KVH * HD), jnp.bfloat16),
        ],
        compiler_params=pltpu.CompilerParams(vmem_limit_bytes=32 * 2**20),
        cost_estimate=pl.CostEstimate(flops=0, bytes_accessed=4 * 2**20, transcendentals=0),
        name="finish",
    )(place, *terms)


def projection_kernel(
    place_ref, *refs
):
    mine_refs, other_refs = refs[:CHIPS], refs[CHIPS : 2 * CHIPS]
    own_ref, far_ref, mine_ref, theirs_ref, tokens, weight, sems = refs[2 * CHIPS :]
    core, a = place_ref[0], place_ref[2]
    pieces = ((own_ref, a), (far_ref, 1 - a))

    copies = [
        pltpu.make_async_copy(
            ref.at[b], weight.at[place * 4 + b], sems.at[i, b]
        )
        for i, (ref, place) in enumerate(pieces)
        for b in range(4)
    ]
    for copy in copies:
        copy.start()
    mine = pl.multiple_of(core * BLOCK, BLOCK)
    others = pl.multiple_of(BLOCK - mine, BLOCK)
    for i in range(CHIPS):
        tokens[pl.ds(i * CHIP + mine, BLOCK), :] = mine_refs[i][...]
        tokens[pl.ds(i * CHIP + others, BLOCK), :] = other_refs[i][...]
    for copy in copies:
        copy.wait()
    depth = SLICES * ROWS
    for i, out_ref in enumerate((mine_ref, theirs_ref)):
        total = jnp.zeros(out_ref.shape, jnp.float32)
        for z in range(SHARDS):
            total += jnp.dot(
                tokens[i * CHIP : (i + 1) * CHIP, z * depth : (z + 1) * depth],
                weight[:, z].reshape(depth, out_ref.shape[1]),
                preferred_element_type=jnp.float32,
            )
        out_ref[...] = total.astype(out_ref.dtype)


def projection(place, mine, other, own, far):
    width = own.shape[-1]
    depth = mine[0].shape[1]
    vmem = pl.BlockSpec(memory_space=pltpu.VMEM)
    away = pl.BlockSpec(memory_space=pl.ANY)
    return pl.pallas_call(
        projection_kernel,
        in_specs=[pl.BlockSpec(memory_space=pltpu.SMEM)] + [vmem] * (2 * CHIPS) + [away] * 2,
        out_specs=[vmem] * 2,
        out_shape=[jax.ShapeDtypeStruct((CHIP, width), jnp.bfloat16)] * 2,
        scratch_shapes=[
            pltpu.VMEM((CHIPS * CHIP, depth), jnp.bfloat16),
            pltpu.VMEM((SLICES, SHARDS, ROWS, width), jnp.bfloat16),
            pltpu.SemaphoreType.DMA((2, 4)),
        ],
        compiler_params=pltpu.CompilerParams(vmem_limit_bytes=32 * 2**20),
        cost_estimate=pl.CostEstimate(
            flops=2 * CHIPS * CHIP * depth * width, bytes_accessed=10 * 2**20, transcendentals=0
        ),
        name="projection",
    )(place, *mine, *other, own, far)


def ring_of(core, x, y, turn, first):
    if (core == 0) == first:
        return x, (y + turn) % 4
    return (x + turn) % 4, y


def number(x, y, core):
    return (x * 4 + y) * CORES + core


def in_plane():
    return [(x, y, core) for x in range(4) for y in range(4) for core in range(CORES)]


def gathered(weight, core, a, b, group):
    piece = lax.dynamic_slice_in_dim(weight, (a * 4 + b) * ROWS, ROWS, 0)
    piece = piece.reshape(ROWS, 2, KVH, HD)
    piece = lax.dynamic_slice_in_dim(piece, core * GROUPS + group, 1, 2).reshape(ROWS, 2 * HD)
    piece = jnp.broadcast_to(piece[None], (SHARDS,) + piece.shape)
    piece = lax.all_to_all(piece, "fsdp", 0, 0)
    groups = {}
    for place in in_plane():
        members = [number(*ring_of(place[2], *place[:2], turn, True), place[2]) for turn in range(4)]
        groups[tuple(sorted(members))] = None
    piece = jnp.broadcast_to(piece[None], (4,) + piece.shape)
    own = lax.all_to_all(piece, "tok", 0, 0, axis_index_groups=[list(g) for g in groups])
    route = [
        (number(*place), number(*ring_of(place[2], *place[:2], 2, False), place[2]))
        for place in in_plane()
    ]
    return own, lax.ppermute(own, "tok", route)


def body(hidden, queries, upstream, context_weight, lengths):
    device = lax.axis_index("tok")
    core, chip = device % CORES, device // CORES

    def along(chip):
        return jnp.where(core == 0, chip // 4, chip % 4)

    a, b = along(chip), jnp.where(core == 0, chip % 4, chip // 4)
    own, opposite = gathered(context_weight, core, a // 2, b, a % 2)

    tokens, traded = [hidden, paired(hidden)], [swapped(hidden), paired(hidden, across=True)]

    queries, upstream, _ = lax.optimization_barrier((queries, upstream, own))
    q_other = swapped(half(queries, 1 - core, 1))
    u_other = swapped(half(upstream, 1 - core, 1))
    kinds = [along(chip) % 2, along(chip + 15) % 2, along(chip + 14) % 2]
    place = jnp.stack([core, chip, a // 2] + kinds).astype(jnp.int32)
    place = jnp.concatenate([place, lengths[0]])
    place, q_other, u_other, opposite = lax.optimization_barrier((place, q_other, u_other, opposite))

    mine, theirs = projection(place, tokens, traded, own, opposite)
    far = [shifted(mine, 2 * CORES), paired(theirs, 2 * CORES)]
    near = [shifted(mine, CORES), paired(theirs, CORES)]
    here = [mine, paired(theirs)]
    (
        log_mine, dq_mine, to_core, here_mine, near_mine, near_other, far_mine, far_other,
    ) = attention(place, queries, q_other, upstream, u_other, *far, *near, *here)
    far_mine, far_other = shifted(far_mine, -2 * CORES), shifted(far_other, -2 * CORES, True)
    near_mine, near_other = shifted(near_mine, -CORES), shifted(near_other, -CORES, True)
    from_core = swapped(to_core)
    return tuple(
        finish(
            place, dq_mine, from_core, log_mine, here_mine, near_mine, far_mine, near_other, far_other
        )
    )


def solution(mesh):
    in_specs = (
        P(("fsdp", "tok"), None),
        P(("fsdp", "tok"), None),
        P(("fsdp", "tok"), None),
        P("fsdp", None),
        P("fsdp", None),
    )
    out_specs = (P(None, ("fsdp", "tok")), P(("fsdp", "tok"), None), P(("fsdp", "tok"), None))
    return jax.shard_map(body, mesh=mesh, in_specs=in_specs, out_specs=out_specs, check_vma=False)
```

```python
import functools
import math

import jax
import jax.numpy as jnp
from jax import lax
from jax.experimental import pallas as pl
from jax.experimental.pallas import tpu as pltpu
from jax.sharding import PartitionSpec as P

QH = 32
KVH = 4
HD = 128
CORES = 2
BLOCK = 128
CHIP = CORES * BLOCK
GROUPS = KVH // CORES
HEADS = QH // KVH
DOCS = 16
LENGTHS = 3
SPAN = 4 * BLOCK
KEYS = SPAN + BLOCK
SHARDS = 16
SLICES = 16
ROWS = 16
SCALE = 1.0 / math.sqrt(HD)
LOG2E = math.log2(math.e)


def shifted(block, distance, across=False):
    count = lax.axis_size("tok")
    route = [(i, i + distance) for i in range(count) if 0 <= i + distance < count]
    if across:
        route = [(i, j ^ 1) for i, j in route]
    return lax.ppermute(block, "tok", route)


def swapped(block):
    count = lax.axis_size("tok")
    return lax.ppermute(block, "tok", [(i, i ^ 1) for i in range(count)])


def half(block, index, axis):
    size = block.shape[axis] // 2
    return lax.dynamic_slice_in_dim(block, index * size, size, axis)


def attention_kernel(
    place_ref, q_mine, q_other, u_mine, u_other, far_ref, near_ref, here_ref,
    log_mine, dq_mine, to_core, here_mine, near_mine, near_other, far_mine, far_other,
    keys, values, sums, bias, q_rows, u_rows, weight_rows, change_rows,
):
    group, part = pl.program_id(0), pl.program_id(1)
    core, chip = place_ref[0], place_ref[1]
    first = pl.multiple_of(jnp.where(part == 0, core, 1 - core) * BLOCK, BLOCK)

    def stack(q_ref, u_ref):
        for head in range(HEADS):
            rows, columns = slice(head * BLOCK, (head + 1) * BLOCK), slice(head * HD, (head + 1) * HD)
            q_rows[rows, :] = q_ref[:, columns]
            u_rows[rows, :] = u_ref[:, columns]

    @pl.when(part == 0)
    def _():
        for i, ref in enumerate((far_ref, near_ref, here_ref)):
            keys[i * CHIP : (i + 1) * CHIP, :] = ref[:, :HD]
            values[i * CHIP : (i + 1) * CHIP, :] = ref[:, HD:]
        sums[...] = jnp.zeros_like(sums)
        stack(q_mine, u_mine)

    @pl.when(part == 1)
    def _():
        stack(q_other, u_other)

    key_window = keys[pl.ds(first, KEYS), :]
    value_window = values[pl.ds(first, KEYS), :]
    places = first - SPAN + lax.broadcasted_iota(jnp.int32, (BLOCK, KEYS), 1)
    own = first + lax.broadcasted_iota(jnp.int32, (BLOCK, KEYS), 0)
    token = first + lax.broadcasted_iota(jnp.int32, (BLOCK, 1), 0)
    start, bound = jnp.zeros((BLOCK, 1), jnp.int32) - chip * CHIP, -chip * CHIP
    for i in range(DOCS):
        bound = bound + place_ref[LENGTHS + i]
        start = jnp.where(token >= bound, bound, start)
    bias[...] = jnp.where((places <= own) & (places >= start), 0.0, -jnp.inf)
    over_rows = (((1,), (1,)), ((), ()))
    dot = functools.partial(jnp.dot, preferred_element_type=jnp.float32)
    dot_rows = functools.partial(
        lax.dot_general, dimension_numbers=over_rows, preferred_element_type=jnp.float32
    )
    count = HEADS // 2
    stripes = [slice(i * count * BLOCK, (i + 1) * count * BLOCK) for i in range(2)]
    scores = [dot_rows(q_rows[rows, :], key_window) for rows in stripes]
    pushed = [dot_rows(u_rows[rows, :], value_window) for rows in stripes]
    weights, logs, attended = [], [], []
    for i, rows in enumerate(stripes):
        masked = scores[i].reshape(count, BLOCK, KEYS) + bias[...][None]
        masked = masked.reshape(count * BLOCK, KEYS)
        highest = jnp.max(masked, axis=1, keepdims=True)
        raised = jnp.exp2((masked - highest) * (SCALE * LOG2E))
        total = jnp.sum(raised, axis=1, keepdims=True)
        logs.append(highest * SCALE + jnp.log(total))
        weights.append(raised * (1.0 / total))
        weight_rows[rows, :] = weights[i].astype(jnp.bfloat16)
        attended.append(dot(weights[i].astype(jnp.bfloat16), value_window).astype(jnp.bfloat16))
    value_slope, key_slope = [], []
    for i, rows in enumerate(stripes):
        product = u_rows[rows, :].astype(jnp.float32) * attended[i].astype(jnp.float32)
        inner = jnp.sum(product, axis=1, keepdims=True)
        change_rows[rows, :] = (weights[i] * (pushed[i] - inner)).astype(jnp.bfloat16)
        value_slope.append(dot(u_rows[rows, :].T, weight_rows[rows, :]))
    slopes = [dot(change_rows[rows, :], key_window) * SCALE for rows in stripes]
    for rows in stripes:
        key_slope.append(dot(q_rows[rows, :].T, change_rows[rows, :]))
    sums[pl.ds(first, KEYS), :HD] += (key_slope[0] + key_slope[1]).T * SCALE
    sums[pl.ds(first, KEYS), HD:] += (value_slope[0] + value_slope[1]).T
    lane = lax.broadcasted_iota(jnp.int32, (BLOCK, HD), 1)
    columns = jnp.zeros((BLOCK, HD), jnp.float32)
    for head in range(HEADS):
        rows = slice(head % count * BLOCK, (head % count + 1) * BLOCK)
        columns = jnp.where(lane % HEADS == head, logs[head // count][rows], columns)

    def head_slope(head):
        rows = slice(head % count * BLOCK, (head % count + 1) * BLOCK)
        return slopes[head // count][rows].astype(jnp.bfloat16)

    @pl.when(part == 0)
    def _():
        log_mine[...] = columns.T[:HEADS]
        for head in range(HEADS):
            dq_mine[:, head * HD : (head + 1) * HD] = head_slope(head)

    @pl.when(part == 1)
    def _():
        high = columns.astype(jnp.bfloat16).astype(jnp.float32)
        middle = (columns - high).astype(jnp.bfloat16).astype(jnp.float32)
        terms = jnp.where(lane < HEADS, high, jnp.where(lane < 2 * HEADS, middle, columns - high - middle))
        mine = pl.multiple_of(core * BLOCK, BLOCK)
        others = pl.multiple_of(BLOCK - mine, BLOCK)

        def rows_of(first, which):
            return sums[pl.ds(first + which, BLOCK), :]

        here_mine[...] = rows_of(SPAN, mine)
        near_mine[...] = rows_of(CHIP, mine).astype(jnp.bfloat16)
        near_other[...] = rows_of(CHIP, others).astype(jnp.bfloat16)
        far_mine[...] = rows_of(0, mine).astype(jnp.bfloat16)
        far_other[...] = rows_of(0, others).astype(jnp.bfloat16)
        here_other = rows_of(SPAN, others).astype(jnp.bfloat16)
        for g in range(GROUPS):

            @pl.when(group == g)
            def _():
                for head in range(HEADS):
                    at = (g * HEADS + head) * HD
                    to_core[:, at : at + HD] = head_slope(head)
                at = GROUPS * HEADS * HD + g * 3 * HD
                to_core[:, at : at + 2 * HD] = here_other
                to_core[:, at + 2 * HD : at + 3 * HD] = terms.astype(jnp.bfloat16)


def attention(place, queries, q_other, upstream, u_other, far, near, here):
    stacked = HEADS * BLOCK
    mine = pl.BlockSpec((BLOCK, HEADS * HD), lambda g, b, place: (0, place[0] * GROUPS + g))
    other = pl.BlockSpec((BLOCK, HEADS * HD), lambda g, b, place: (0, g))
    context = pl.BlockSpec((CHIP, 2 * HD), lambda g, b, place: (0, g))
    block = pl.BlockSpec((BLOCK, 2 * HD), lambda g, b, place: (0, g))
    log = pl.BlockSpec((HEADS, BLOCK), lambda g, b, place: (g, 0))
    wide, packed, heads = GROUPS * 2 * HD, GROUPS * 3 * HD, GROUPS * HEADS
    term = jax.ShapeDtypeStruct((BLOCK, wide), jnp.bfloat16)
    return pl.pallas_call(
        attention_kernel,
        grid_spec=pltpu.PrefetchScalarGridSpec(
            num_scalar_prefetch=1,
            grid=(GROUPS, CORES),
            in_specs=[
                mine, other, mine, other, context, context, context,
            ],
            out_specs=[
                log, other,
                pl.BlockSpec((BLOCK, heads * HD + packed), lambda g, b, place: (0, 0)),
                block, block, block, block, block,
            ],
            scratch_shapes=[
                pltpu.VMEM((SPAN + CHIP, HD), jnp.bfloat16),
                pltpu.VMEM((SPAN + CHIP, HD), jnp.bfloat16),
                pltpu.VMEM((SPAN + CHIP, 2 * HD), jnp.float32),
                pltpu.VMEM((BLOCK, KEYS), jnp.float32),
                pltpu.VMEM((stacked, HD), jnp.bfloat16),
                pltpu.VMEM((stacked, HD), jnp.bfloat16),
                pltpu.VMEM((stacked, KEYS), jnp.bfloat16),
                pltpu.VMEM((stacked, KEYS), jnp.bfloat16),
            ],
        ),
        out_shape=[
            jax.ShapeDtypeStruct((heads, BLOCK), jnp.float32),
            jax.ShapeDtypeStruct((BLOCK, heads * HD), jnp.bfloat16),
            jax.ShapeDtypeStruct((BLOCK, heads * HD + packed), jnp.bfloat16),
            jax.ShapeDtypeStruct((BLOCK, wide), jnp.float32),
            term, term, term, term,
        ],
        compiler_params=pltpu.CompilerParams(vmem_limit_bytes=48 * 2**20),
        cost_estimate=pl.CostEstimate(
            flops=12 * CHIP * KEYS * HD * GROUPS * HEADS,
            bytes_accessed=8 * 2**20,
            transcendentals=CHIP * KEYS * GROUPS * HEADS,
        ),
        name="attention",
    )(place, queries, q_other, upstream, u_other, far, near, here)


def finish_kernel(
    place_ref, dq_mine, from_core, log_mine, here_mine, near_mine, far_mine, near_other, far_other,
    log_ref, dq_ref, context_ref,
):
    width, heads = dq_mine.shape[1], log_mine.shape[0]

    def put(which, dq, log, slopes):
        dq_ref[:, which * width : (which + 1) * width] = dq
        for g in range(GROUPS):
            row = which * heads + g * HEADS
            log_ref[row : row + HEADS, :] = log[g]
            for kind in range(2):
                to = (kind * KVH + which * GROUPS + g) * HD
                context_ref[:, to : to + HD] = slopes[g][:, kind * HD : (kind + 1) * HD]

    def total(here, near, far, g):
        at = slice(g * 2 * HD, (g + 1) * 2 * HD)
        terms = here + near[:, at].astype(jnp.float32) + far[:, at].astype(jnp.float32)
        return terms.astype(jnp.bfloat16)

    mine, other, logs = [], [], []
    for g in range(GROUPS):
        at = width + g * 3 * HD
        mine.append(total(here_mine[:, g * 2 * HD : (g + 1) * 2 * HD], near_mine, far_mine, g))
        here = from_core[:, at : at + 2 * HD].astype(jnp.float32)
        other.append(total(here, near_other, far_other, g))
        terms = from_core[:, at + 2 * HD : at + 3 * HD].astype(jnp.float32).T
        logs.append(terms[:HEADS] + terms[HEADS : 2 * HEADS] + terms[2 * HEADS : 3 * HEADS])
    own_logs = [log_mine[g * HEADS : (g + 1) * HEADS, :] for g in range(GROUPS)]
    for core in range(CORES):

        @pl.when(place_ref[0] == core)
        def _():
            put(core, dq_mine[...], own_logs, mine)
            put(1 - core, from_core[:, :width], logs, other)


def finish(place, *terms):
    vmem = pl.BlockSpec(memory_space=pltpu.VMEM)
    return pl.pallas_call(
        finish_kernel,
        in_specs=[pl.BlockSpec(memory_space=pltpu.SMEM)] + [vmem] * len(terms),
        out_specs=[vmem] * 3,
        out_shape=[
            jax.ShapeDtypeStruct((QH, BLOCK), jnp.float32),
            jax.ShapeDtypeStruct((BLOCK, QH * HD), jnp.bfloat16),
            jax.ShapeDtypeStruct((BLOCK, 2 * KVH * HD), jnp.bfloat16),
        ],
        compiler_params=pltpu.CompilerParams(vmem_limit_bytes=32 * 2**20),
        cost_estimate=pl.CostEstimate(flops=0, bytes_accessed=4 * 2**20, transcendentals=0),
        name="finish",
    )(place, *terms)


def projection_kernel(
    place_ref, mine_ref, other_ref, own_ref, left_ref, right_ref, far_ref, out_ref, tokens, weight, sems
):
    core, a = place_ref[0], place_ref[2]
    pieces = ((own_ref, 0), (left_ref, 3), (right_ref, 1), (far_ref, 2))

    copies = [
        pltpu.make_async_copy(
            ref.at[b], weight.at[lax.rem(a + turn, 4) * 4 + b], sems.at[i, b]
        )
        for i, (ref, turn) in enumerate(pieces)
        for b in range(4)
    ]
    for copy in copies:
        copy.start()
    mine = pl.multiple_of(core * BLOCK, BLOCK)
    tokens[pl.ds(mine, BLOCK), :] = mine_ref[...]
    tokens[pl.ds(BLOCK - mine, BLOCK), :] = other_ref[...]
    for copy in copies:
        copy.wait()
    total = jnp.zeros(out_ref.shape, jnp.float32)
    depth = SLICES * ROWS
    for z in range(SHARDS):
        total += jnp.dot(
            tokens[:, z * depth : (z + 1) * depth],
            weight[:, z].reshape(depth, out_ref.shape[1]),
            preferred_element_type=jnp.float32,
        )
    out_ref[...] = total.astype(out_ref.dtype)


def projection(place, mine, other, own, left, right, far):
    width = own.shape[-1]
    depth = mine.shape[1]
    vmem = pl.BlockSpec(memory_space=pltpu.VMEM)
    away = pl.BlockSpec(memory_space=pl.ANY)
    return pl.pallas_call(
        projection_kernel,
        in_specs=[pl.BlockSpec(memory_space=pltpu.SMEM), vmem, vmem, away, away, away, away],
        out_specs=vmem,
        out_shape=jax.ShapeDtypeStruct((CHIP, width), jnp.bfloat16),
        scratch_shapes=[
            pltpu.VMEM((CHIP, depth), jnp.bfloat16),
            pltpu.VMEM((SLICES, SHARDS, ROWS, width), jnp.bfloat16),
            pltpu.SemaphoreType.DMA((4, 4)),
        ],
        compiler_params=pltpu.CompilerParams(vmem_limit_bytes=32 * 2**20),
        cost_estimate=pl.CostEstimate(
            flops=2 * CHIP * depth * width, bytes_accessed=6 * 2**20, transcendentals=0
        ),
        name="projection",
    )(place, mine, other, own, left, right, far)


def ring_of(core, x, y, turn, first):
    if (core == 0) == first:
        return x, (y + turn) % 4
    return (x + turn) % 4, y


def number(x, y, core):
    return (x * 4 + y) * CORES + core


def in_plane():
    return [(x, y, core) for x in range(4) for y in range(4) for core in range(CORES)]


def gathered(weight, device):
    chip, core = device // CORES, device % CORES
    x, y = chip // 4, chip % 4
    a, b = jnp.where(core == 0, x, y), jnp.where(core == 0, y, x)
    piece = lax.dynamic_slice_in_dim(weight, (a * 4 + b) * ROWS, ROWS, 0)
    piece = piece.reshape(ROWS, 2, CORES, GROUPS, HD)
    piece = lax.dynamic_slice_in_dim(piece, core, 1, 2)[:, :, 0]
    piece = piece.transpose(0, 2, 1, 3).reshape(ROWS, GROUPS * 2 * HD)
    piece = jnp.broadcast_to(piece[None], (SHARDS,) + piece.shape)
    first = lax.all_to_all(piece, "fsdp", 0, 0)
    groups = {}
    for place in in_plane():
        members = [number(*ring_of(place[2], *place[:2], turn, True), place[2]) for turn in range(4)]
        groups[tuple(sorted(members))] = None
    piece = jnp.broadcast_to(first[None], (4,) + first.shape)
    own = lax.all_to_all(piece, "tok", 0, 0, axis_index_groups=[list(g) for g in groups])

    def turned(turn):
        route = [
            (number(*place), number(*ring_of(place[2], *place[:2], turn, False), place[2]))
            for place in in_plane()
        ]
        return lax.ppermute(own, "tok", route)

    return a, first, own, turned(1), turned(-1), turned(2)


def body(hidden, queries, upstream, context_weight, lengths):
    device = lax.axis_index("tok")
    core, chip = device % CORES, device // CORES
    a, first, own, left, right, opposite = gathered(context_weight, device)

    hidden, queries, upstream, _ = lax.optimization_barrier((hidden, queries, upstream, first))
    other_hidden = swapped(hidden)
    q_other = swapped(half(queries, 1 - core, 1))
    u_other = swapped(half(upstream, 1 - core, 1))
    place = jnp.concatenate([jnp.stack([core, chip, a]).astype(jnp.int32), lengths[0]])
    place, q_other, u_other, opposite = lax.optimization_barrier((place, q_other, u_other, opposite))

    here = projection(place, hidden, other_hidden, own, left, right, opposite)
    near = shifted(here, CORES)
    far = shifted(here, 2 * CORES)
    (
        log_mine, dq_mine, to_core, here_mine, near_mine, near_other, far_mine, far_other,
    ) = attention(place, queries, q_other, upstream, u_other, far, near, here)
    far_mine, far_other = shifted(far_mine, -2 * CORES), shifted(far_other, -2 * CORES, True)
    near_mine, near_other = shifted(near_mine, -CORES), shifted(near_other, -CORES, True)
    from_core = swapped(to_core)
    return tuple(
        finish(
            place, dq_mine, from_core, log_mine, here_mine, near_mine, far_mine, near_other, far_other
        )
    )


def solution(mesh):
    in_specs = (
        P(("fsdp", "tok"), None),
        P(("fsdp", "tok"), None),
        P(("fsdp", "tok"), None),
        P("fsdp", None),
        P("fsdp", None),
    )
    out_specs = (P(None, ("fsdp", "tok")), P(("fsdp", "tok"), None), P(("fsdp", "tok"), None))
    return jax.shard_map(body, mesh=mesh, in_specs=in_specs, out_specs=out_specs, check_vma=False)
```

```python
import functools
import math

import jax
import jax.numpy as jnp
from jax import lax
from jax.experimental import pallas as pl
from jax.experimental.pallas import tpu as pltpu
from jax.sharding import PartitionSpec as P

QH = 32
KVH = 4
HD = 128
CORES = 2
BLOCK = 128
CHIP = CORES * BLOCK
GROUPS = KVH // CORES
HEADS = QH // KVH
DOCS = 16
LENGTHS = 3
SPAN = 4 * BLOCK
KEYS = SPAN + BLOCK
SHARDS = 16
SLICES = 16
ROWS = 16
PARTS = 2
SCALE = 1.0 / math.sqrt(HD)
LOG2E = math.log2(math.e)


def shifted(block, distance, across=False):
    count = lax.axis_size("tok")
    route = [(i, i + distance) for i in range(count) if 0 <= i + distance < count]
    if across:
        route = [(i, j ^ 1) for i, j in route]
    return lax.ppermute(block, "tok", route)


def swapped(block):
    count = lax.axis_size("tok")
    return lax.ppermute(block, "tok", [(i, i ^ 1) for i in range(count)])


def half(block, index, axis):
    size = block.shape[axis] // 2
    return lax.dynamic_slice_in_dim(block, index * size, size, axis)


def attention_kernel(
    place_ref, q_mine, q_other, u_mine, u_other, far_ref, near_ref, here_ref,
    log_mine, dq_mine, to_core, here_mine, near_mine, near_other, far_mine, far_other,
    keys, values, sums, bias, q_rows, u_rows, weight_rows, change_rows,
):
    group, part = pl.program_id(0), pl.program_id(1)
    core, chip = place_ref[0], place_ref[1]
    first = pl.multiple_of(jnp.where(part == 0, core, 1 - core) * BLOCK, BLOCK)

    def stack(q_ref, u_ref):
        for head in range(HEADS):
            rows, columns = slice(head * BLOCK, (head + 1) * BLOCK), slice(head * HD, (head + 1) * HD)
            q_rows[rows, :] = q_ref[:, columns]
            u_rows[rows, :] = u_ref[:, columns]

    @pl.when(part == 0)
    def _():
        for i, ref in enumerate((far_ref, near_ref, here_ref)):
            keys[i * CHIP : (i + 1) * CHIP, :] = ref[:, :HD]
            values[i * CHIP : (i + 1) * CHIP, :] = ref[:, HD:]
        sums[...] = jnp.zeros_like(sums)
        stack(q_mine, u_mine)

    @pl.when(part == 1)
    def _():
        stack(q_other, u_other)

    key_window = keys[pl.ds(first, KEYS), :]
    value_window = values[pl.ds(first, KEYS), :]
    places = first - SPAN + lax.broadcasted_iota(jnp.int32, (BLOCK, KEYS), 1)
    own = first + lax.broadcasted_iota(jnp.int32, (BLOCK, KEYS), 0)
    token = first + lax.broadcasted_iota(jnp.int32, (BLOCK, 1), 0)
    start, bound = jnp.zeros((BLOCK, 1), jnp.int32) - chip * CHIP, -chip * CHIP
    for i in range(DOCS):
        bound = bound + place_ref[LENGTHS + i]
        start = jnp.where(token >= bound, bound, start)
    bias[...] = jnp.where((places <= own) & (places >= start), 0.0, -jnp.inf)
    over_rows = (((1,), (1,)), ((), ()))
    dot = functools.partial(jnp.dot, preferred_element_type=jnp.float32)
    dot_rows = functools.partial(
        lax.dot_general, dimension_numbers=over_rows, preferred_element_type=jnp.float32
    )
    count = HEADS // 2
    stripes = [slice(i * count * BLOCK, (i + 1) * count * BLOCK) for i in range(2)]
    scores = [dot_rows(q_rows[rows, :], key_window) for rows in stripes]
    pushed = [dot_rows(u_rows[rows, :], value_window) for rows in stripes]
    weights, logs, attended = [], [], []
    for i, rows in enumerate(stripes):
        masked = scores[i].reshape(count, BLOCK, KEYS) + bias[...][None]
        masked = masked.reshape(count * BLOCK, KEYS)
        highest = jnp.max(masked, axis=1, keepdims=True)
        raised = jnp.exp2((masked - highest) * (SCALE * LOG2E))
        total = jnp.sum(raised, axis=1, keepdims=True)
        logs.append(highest * SCALE + jnp.log(total))
        weights.append(raised * (1.0 / total))
        weight_rows[rows, :] = weights[i].astype(jnp.bfloat16)
        attended.append(dot(weights[i].astype(jnp.bfloat16), value_window).astype(jnp.bfloat16))
    value_slope, key_slope = [], []
    for i, rows in enumerate(stripes):
        product = u_rows[rows, :].astype(jnp.float32) * attended[i].astype(jnp.float32)
        inner = jnp.sum(product, axis=1, keepdims=True)
        change_rows[rows, :] = (weights[i] * (pushed[i] - inner)).astype(jnp.bfloat16)
        value_slope.append(dot(u_rows[rows, :].T, weight_rows[rows, :]))
    slopes = [dot(change_rows[rows, :], key_window) * SCALE for rows in stripes]
    for rows in stripes:
        key_slope.append(dot(q_rows[rows, :].T, change_rows[rows, :]))
    sums[pl.ds(first, KEYS), :HD] += (key_slope[0] + key_slope[1]).T * SCALE
    sums[pl.ds(first, KEYS), HD:] += (value_slope[0] + value_slope[1]).T
    lane = lax.broadcasted_iota(jnp.int32, (BLOCK, HD), 1)
    columns = jnp.zeros((BLOCK, HD), jnp.float32)
    for head in range(HEADS):
        rows = slice(head % count * BLOCK, (head % count + 1) * BLOCK)
        columns = jnp.where(lane % HEADS == head, logs[head // count][rows], columns)

    def head_slope(head):
        rows = slice(head % count * BLOCK, (head % count + 1) * BLOCK)
        return slopes[head // count][rows].astype(jnp.bfloat16)

    @pl.when(part == 0)
    def _():
        log_mine[...] = columns.T[:HEADS]
        for head in range(HEADS):
            dq_mine[:, head * HD : (head + 1) * HD] = head_slope(head)

    @pl.when(part == 1)
    def _():
        high = columns.astype(jnp.bfloat16).astype(jnp.float32)
        middle = (columns - high).astype(jnp.bfloat16).astype(jnp.float32)
        terms = jnp.where(lane < HEADS, high, jnp.where(lane < 2 * HEADS, middle, columns - high - middle))
        mine = pl.multiple_of(core * BLOCK, BLOCK)
        others = pl.multiple_of(BLOCK - mine, BLOCK)

        def rows_of(first, which):
            return sums[pl.ds(first + which, BLOCK), :]

        here_mine[...] = rows_of(SPAN, mine)
        near_mine[...] = rows_of(CHIP, mine).astype(jnp.bfloat16)
        near_other[...] = rows_of(CHIP, others).astype(jnp.bfloat16)
        far_mine[...] = rows_of(0, mine).astype(jnp.bfloat16)
        far_other[...] = rows_of(0, others).astype(jnp.bfloat16)
        here_other = rows_of(SPAN, others).astype(jnp.bfloat16)
        for g in range(GROUPS):

            @pl.when(group == g)
            def _():
                for head in range(HEADS):
                    at = (g * HEADS + head) * HD
                    to_core[:, at : at + HD] = head_slope(head)
                at = GROUPS * HEADS * HD + g * 3 * HD
                to_core[:, at : at + 2 * HD] = here_other
                to_core[:, at + 2 * HD : at + 3 * HD] = terms.astype(jnp.bfloat16)


def attention(place, queries, q_other, upstream, u_other, far, near, here):
    stacked = HEADS * BLOCK
    mine = pl.BlockSpec((BLOCK, HEADS * HD), lambda g, b, place: (0, place[0] * GROUPS + g))
    other = pl.BlockSpec((BLOCK, HEADS * HD), lambda g, b, place: (0, g))
    context = pl.BlockSpec((CHIP, 2 * HD), lambda g, b, place: (0, g))
    block = pl.BlockSpec((BLOCK, 2 * HD), lambda g, b, place: (0, g))
    log = pl.BlockSpec((HEADS, BLOCK), lambda g, b, place: (g, 0))
    wide, packed, heads = GROUPS * 2 * HD, GROUPS * 3 * HD, GROUPS * HEADS
    term = jax.ShapeDtypeStruct((BLOCK, wide), jnp.bfloat16)
    return pl.pallas_call(
        attention_kernel,
        grid_spec=pltpu.PrefetchScalarGridSpec(
            num_scalar_prefetch=1,
            grid=(GROUPS, CORES),
            in_specs=[
                mine, other, mine, other, context, context, context,
            ],
            out_specs=[
                log, other,
                pl.BlockSpec((BLOCK, heads * HD + packed), lambda g, b, place: (0, 0)),
                block, block, block, block, block,
            ],
            scratch_shapes=[
                pltpu.VMEM((SPAN + CHIP, HD), jnp.bfloat16),
                pltpu.VMEM((SPAN + CHIP, HD), jnp.bfloat16),
                pltpu.VMEM((SPAN + CHIP, 2 * HD), jnp.float32),
                pltpu.VMEM((BLOCK, KEYS), jnp.float32),
                pltpu.VMEM((stacked, HD), jnp.bfloat16),
                pltpu.VMEM((stacked, HD), jnp.bfloat16),
                pltpu.VMEM((stacked, KEYS), jnp.bfloat16),
                pltpu.VMEM((stacked, KEYS), jnp.bfloat16),
            ],
        ),
        out_shape=[
            jax.ShapeDtypeStruct((heads, BLOCK), jnp.float32),
            jax.ShapeDtypeStruct((BLOCK, heads * HD), jnp.bfloat16),
            jax.ShapeDtypeStruct((BLOCK, heads * HD + packed), jnp.bfloat16),
            jax.ShapeDtypeStruct((BLOCK, wide), jnp.float32),
            term, term, term, term,
        ],
        compiler_params=pltpu.CompilerParams(vmem_limit_bytes=48 * 2**20),
        cost_estimate=pl.CostEstimate(
            flops=12 * CHIP * KEYS * HD * GROUPS * HEADS,
            bytes_accessed=8 * 2**20,
            transcendentals=CHIP * KEYS * GROUPS * HEADS,
        ),
        name="attention",
    )(place, queries, q_other, upstream, u_other, far, near, here)


def finish_kernel(
    place_ref, dq_mine, from_core, log_mine, here_mine, near_mine, far_mine, near_other, far_other,
    log_ref, dq_ref, context_ref,
):
    width, heads = dq_mine.shape[1], log_mine.shape[0]

    def put(which, dq, log, slopes):
        dq_ref[:, which * width : (which + 1) * width] = dq
        for g in range(GROUPS):
            row = which * heads + g * HEADS
            log_ref[row : row + HEADS, :] = log[g]
            for kind in range(2):
                to = (kind * KVH + which * GROUPS + g) * HD
                context_ref[:, to : to + HD] = slopes[g][:, kind * HD : (kind + 1) * HD]

    def total(here, near, far, g):
        at = slice(g * 2 * HD, (g + 1) * 2 * HD)
        terms = here + near[:, at].astype(jnp.float32) + far[:, at].astype(jnp.float32)
        return terms.astype(jnp.bfloat16)

    mine, other, logs = [], [], []
    for g in range(GROUPS):
        at = width + g * 3 * HD
        mine.append(total(here_mine[:, g * 2 * HD : (g + 1) * 2 * HD], near_mine, far_mine, g))
        here = from_core[:, at : at + 2 * HD].astype(jnp.float32)
        other.append(total(here, near_other, far_other, g))
        terms = from_core[:, at + 2 * HD : at + 3 * HD].astype(jnp.float32).T
        logs.append(terms[:HEADS] + terms[HEADS : 2 * HEADS] + terms[2 * HEADS : 3 * HEADS])
    own_logs = [log_mine[g * HEADS : (g + 1) * HEADS, :] for g in range(GROUPS)]
    for core in range(CORES):

        @pl.when(place_ref[0] == core)
        def _():
            put(core, dq_mine[...], own_logs, mine)
            put(1 - core, from_core[:, :width], logs, other)


def finish(place, *terms):
    vmem = pl.BlockSpec(memory_space=pltpu.VMEM)
    return pl.pallas_call(
        finish_kernel,
        in_specs=[pl.BlockSpec(memory_space=pltpu.SMEM)] + [vmem] * len(terms),
        out_specs=[vmem] * 3,
        out_shape=[
            jax.ShapeDtypeStruct((QH, BLOCK), jnp.float32),
            jax.ShapeDtypeStruct((BLOCK, QH * HD), jnp.bfloat16),
            jax.ShapeDtypeStruct((BLOCK, 2 * KVH * HD), jnp.bfloat16),
        ],
        compiler_params=pltpu.CompilerParams(vmem_limit_bytes=32 * 2**20),
        cost_estimate=pl.CostEstimate(flops=0, bytes_accessed=4 * 2**20, transcendentals=0),
        name="finish",
    )(place, *terms)


def projection_kernel(
    place_ref, mine_ref, other_ref, own_ref, left_ref, right_ref, far_ref, out_ref, tokens, weight, sems
):
    core, a = place_ref[0], place_ref[2]
    pieces = ((own_ref, 0), (left_ref, 3), (right_ref, 1), (far_ref, 2))

    step = SHARDS // PARTS
    copies = [
        [
            pltpu.make_async_copy(
                ref.at[b, pl.ds(part * step, step)],
                weight.at[lax.rem(a + turn, 4) * 4 + b, pl.ds(part * step, step)],
                sems.at[part, i, b],
            )
            for i, (ref, turn) in enumerate(pieces)
            for b in range(4)
        ]
        for part in range(PARTS)
    ]
    for part in copies:
        for copy in part:
            copy.start()
    mine = pl.multiple_of(core * BLOCK, BLOCK)
    tokens[pl.ds(mine, BLOCK), :] = mine_ref[...]
    tokens[pl.ds(BLOCK - mine, BLOCK), :] = other_ref[...]
    total = jnp.zeros(out_ref.shape, jnp.float32)
    depth = SLICES * ROWS
    for z in range(SHARDS):
        if z % step == 0:
            for copy in copies[z // step]:
                copy.wait()
        total += jnp.dot(
            tokens[:, z * depth : (z + 1) * depth],
            weight[:, z].reshape(depth, out_ref.shape[1]),
            preferred_element_type=jnp.float32,
        )
    out_ref[...] = total.astype(out_ref.dtype)


def projection(place, mine, other, own, left, right, far):
    width = own.shape[-1]
    depth = mine.shape[1]
    vmem = pl.BlockSpec(memory_space=pltpu.VMEM)
    away = pl.BlockSpec(memory_space=pl.ANY)
    return pl.pallas_call(
        projection_kernel,
        in_specs=[pl.BlockSpec(memory_space=pltpu.SMEM), vmem, vmem, away, away, away, away],
        out_specs=vmem,
        out_shape=jax.ShapeDtypeStruct((CHIP, width), jnp.bfloat16),
        scratch_shapes=[
            pltpu.VMEM((CHIP, depth), jnp.bfloat16),
            pltpu.VMEM((SLICES, SHARDS, ROWS, width), jnp.bfloat16),
            pltpu.SemaphoreType.DMA((PARTS, 4, 4)),
        ],
        compiler_params=pltpu.CompilerParams(vmem_limit_bytes=32 * 2**20),
        cost_estimate=pl.CostEstimate(
            flops=2 * CHIP * depth * width, bytes_accessed=6 * 2**20, transcendentals=0
        ),
        name="projection",
    )(place, mine, other, own, left, right, far)


def ring_of(core, x, y, turn, first):
    if (core == 0) == first:
        return x, (y + turn) % 4
    return (x + turn) % 4, y


def number(x, y, core):
    return (x * 4 + y) * CORES + core


def in_plane():
    return [(x, y, core) for x in range(4) for y in range(4) for core in range(CORES)]


def gathered(weight, device):
    chip, core = device // CORES, device % CORES
    x, y = chip // 4, chip % 4
    a, b = jnp.where(core == 0, x, y), jnp.where(core == 0, y, x)
    piece = lax.dynamic_slice_in_dim(weight, (a * 4 + b) * ROWS, ROWS, 0)
    piece = piece.reshape(ROWS, 2, CORES, GROUPS, HD)
    piece = lax.dynamic_slice_in_dim(piece, core, 1, 2)[:, :, 0]
    piece = piece.transpose(0, 2, 1, 3).reshape(ROWS, GROUPS * 2 * HD)
    piece = jnp.broadcast_to(piece[None], (SHARDS,) + piece.shape)
    first = lax.all_to_all(piece, "fsdp", 0, 0)
    groups = {}
    for place in in_plane():
        members = [number(*ring_of(place[2], *place[:2], turn, True), place[2]) for turn in range(4)]
        groups[tuple(sorted(members))] = None
    piece = jnp.broadcast_to(first[None], (4,) + first.shape)
    own = lax.all_to_all(piece, "tok", 0, 0, axis_index_groups=[list(g) for g in groups])

    def turned(turn):
        route = [
            (number(*place), number(*ring_of(place[2], *place[:2], turn, False), place[2]))
            for place in in_plane()
        ]
        return lax.ppermute(own, "tok", route)

    return a, first, own, turned(1), turned(-1), turned(2)


def body(hidden, queries, upstream, context_weight, lengths):
    device = lax.axis_index("tok")
    core, chip = device % CORES, device // CORES
    a, first, own, left, right, opposite = gathered(context_weight, device)

    hidden, queries, upstream, _ = lax.optimization_barrier((hidden, queries, upstream, first))
    other_hidden = swapped(hidden)
    q_other = swapped(half(queries, 1 - core, 1))
    u_other = swapped(half(upstream, 1 - core, 1))
    place = jnp.concatenate([jnp.stack([core, chip, a]).astype(jnp.int32), lengths[0]])
    place, q_other, u_other, opposite = lax.optimization_barrier((place, q_other, u_other, opposite))

    here = projection(place, hidden, other_hidden, own, left, right, opposite)
    near = shifted(here, CORES)
    far = shifted(here, 2 * CORES)
    (
        log_mine, dq_mine, to_core, here_mine, near_mine, near_other, far_mine, far_other,
    ) = attention(place, queries, q_other, upstream, u_other, far, near, here)
    far_mine, far_other = shifted(far_mine, -2 * CORES), shifted(far_other, -2 * CORES, True)
    near_mine, near_other = shifted(near_mine, -CORES), shifted(near_other, -CORES, True)
    from_core = swapped(to_core)
    return tuple(
        finish(
            place, dq_mine, from_core, log_mine, here_mine, near_mine, far_mine, near_other, far_other
        )
    )


def solution(mesh):
    in_specs = (
        P(("fsdp", "tok"), None),
        P(("fsdp", "tok"), None),
        P(("fsdp", "tok"), None),
        P("fsdp", None),
        P("fsdp", None),
    )
    out_specs = (P(None, ("fsdp", "tok")), P(("fsdp", "tok"), None), P(("fsdp", "tok"), None))
    return jax.shard_map(body, mesh=mesh, in_specs=in_specs, out_specs=out_specs, check_vma=False)
```
